128 devices in a mesh: pole: 4 (over x_lo, core), tile: 32 (over y, x_hi, z).
Axes of the slice: x: 4 (x_hi: 2, x_lo: 2; x = x_hi * 2 + x_lo), y: 4, z: 4, core: 2. Of those that a mesh axis runs over, the one named last changes fastest.
Arguments:
- psi: float32 [2, 1024, 16, 512], P(None, 'tile', None, 'pole'), may hold values from 0 to 3
- trap: float32 [1024, 16, 512], P('tile', None, 'pole'), may hold values from 0 to 2
- pole_shift: float32 [8, 2], P('pole'), may hold values from 1 to 3
- pole_weight: float32 [8, 2], P('pole'), may hold values from -1 to 1
Outputs:
- evolved: float32 [2, 1024, 16, 512], P(None, 'tile', None, 'pole')
The draws below stay inside these ranges and needn't reach their ends.
All inputs are finite; a program needn't handle non-finite values.
Results may differ from the reference program's by a relative error of at most 0.0003.
Values sent between devices are 32-bit elements; how exact they have to be, the bound alone decides.
No kernel may reach another device: no remote copies, remote signals or barrier semaphores. Data moves between devices by JAX's collectives and lax.ppermute only.
A program may use at most 128 MiB of HBM per device.

```python
import jax
import jax.numpy as jnp

NZ = 16
ITERS = 3
POLES = 8
NX = 1024
NY = 512


def draw_psi(key, part):
    key = jax.random.fold_in(key, 11)
    values = jax.random.uniform(key, (2, NX, NZ, NY), jnp.float32, 0.5, 1.5)
    profile = 0.6 + 1.2 * (jnp.arange(NX, dtype=jnp.float32) + 0.5) / NX
    return values * profile[None, :, None, None]


def level_of(own_key, dims, split, low, top_value):
    level = 1.0
    for axis_at, blocks in split:
        steps = jax.random.uniform(jax.random.fold_in(jax.random.fold_in(own_key, 6), axis_at), (blocks,), jnp.float32, low / len(split), top_value / len(split))
        level = level * jnp.repeat(jnp.exp(steps), dims[axis_at] // blocks).reshape((-1,) + (1,) * (len(dims) - 1 - axis_at))
    return level


def setup_inputs(seed: int = 0) -> dict:
    arg_keys = jax.random.split(jax.random.key(seed), 5)
    psi = draw_psi(jax.random.fold_in(arg_keys[4], 71), 0)
    trap = jnp.clip(2.0 * jax.random.uniform(arg_keys[1], (NX, NZ, NY), jnp.float32) ** level_of(arg_keys[1], (NX, NZ, NY), ((0, 32), (2, 4)), -0.2, 0.2), 0.0, 2.0)
    pole_shift = jnp.clip(1.0 + 2.0 * jax.random.uniform(arg_keys[2], (POLES, 2), jnp.float32) ** level_of(arg_keys[2], (POLES, 2), ((0, 4),), -0.2, 0.2), 1.0, 3.0)
    pole_weight = jnp.clip(jax.random.uniform(arg_keys[3], (POLES, 2), jnp.float32, -1.0, 1.0) * level_of(arg_keys[3], (POLES, 2), ((0, 4),), -0.4, 0.0), -1.0, 1.0)
    return {"psi": psi, "trap": trap, "pole_shift": pole_shift, "pole_weight": pole_weight}


COUPLING = 0.5
TIME_STEP = 0.25
WEIGHT_CENTRE = -128.0 / 30.0
WEIGHT_FACE = 14.0 / 30.0
WEIGHT_EDGE = 3.0 / 30.0
WEIGHT_CORNER = 1.0 / 30.0


def laplace(extended):
    padded = jnp.pad(extended, ((0, 0), (0, 0), (0, 0), (1, 1), (1, 1)))
    edges = padded[:, :, :, :-2, 1:-1] + padded[:, :, :, 2:, 1:-1] + padded[:, :, :, 1:-1, :-2] + padded[:, :, :, 1:-1, 2:]
    corners = padded[:, :, :, :-2, :-2] + padded[:, :, :, :-2, 2:] + padded[:, :, :, 2:, :-2] + padded[:, :, :, 2:, 2:]
    in_plane = WEIGHT_CENTRE * extended + WEIGHT_FACE * edges + WEIGHT_EDGE * corners
    off_plane = WEIGHT_FACE * extended + WEIGHT_EDGE * edges + WEIGHT_CORNER * corners
    return in_plane[:, :, 1:-1] + off_plane[:, :, :-2] + off_plane[:, :, 2:]


def operate(extended, potential, shift_re, shift_im):
    current = extended[:, :, 1:-1]
    kinetic = -0.5 * laplace(extended) + potential * current
    real_part = shift_re * current[:, 0] - shift_im * current[:, 1] - TIME_STEP * kinetic[:, 1]
    imag_part = shift_re * current[:, 1] + shift_im * current[:, 0] + TIME_STEP * kinetic[:, 0]
    return jnp.stack([real_part, imag_part], axis=1)


def bilinear_terms(left, right):
    real_sum = jnp.sum(left[:, 0] * right[:, 0] - left[:, 1] * right[:, 1], axis=(1, 2, 3))
    imag_sum = jnp.sum(left[:, 0] * right[:, 1] + left[:, 1] * right[:, 0], axis=(1, 2, 3))
    return real_sum, imag_sum


def divide(numer, denom):
    norm_sq = denom[0] * denom[0] + denom[1] * denom[1]
    return (numer[0] * denom[0] + numer[1] * denom[1]) / norm_sq, (numer[1] * denom[0] - numer[0] * denom[1]) / norm_sq


def scaled(coef, vector):
    coef_re = coef[0][:, None, None, None]
    coef_im = coef[1][:, None, None, None]
    return jnp.stack([coef_re * vector[:, 0] - coef_im * vector[:, 1], coef_re * vector[:, 1] + coef_im * vector[:, 0]], axis=1)


def solve_pole(rhs, potential, shift_re, shift_im):
    def apply_operator(direction):
        extended = jnp.pad(direction, ((0, 0), (0, 0), (1, 1), (0, 0), (0, 0)))
        return operate(extended, potential, shift_re, shift_im)

    iterate = jnp.zeros_like(rhs)
    remain = rhs
    search = rhs
    rho = bilinear_terms(remain, remain)
    for step in range(ITERS):
        image = apply_operator(search)
        alpha = divide(rho, bilinear_terms(search, image))
        iterate = iterate + scaled(alpha, search)
        remain = remain - scaled(alpha, image)
        if step + 1 < ITERS:
            rho_next = bilinear_terms(remain, remain)
            beta = divide(rho_next, rho)
            search = remain + scaled(beta, search)
            rho = rho_next
    return iterate


def reference(psi, trap, pole_shift, pole_weight):
    potential = trap + COUPLING * (psi[0] * psi[0] + psi[1] * psi[1])
    rhs = psi[None]
    evolved = jnp.zeros(psi.shape, jnp.float32)
    for index in range(POLES):
        shift_re = pole_shift[index:index + 1, 0][:, None, None, None]
        shift_im = pole_shift[index:index + 1, 1][:, None, None, None]
        solution = solve_pole(rhs, potential, shift_re, shift_im)
        weight = (pole_weight[index:index + 1, 0], pole_weight[index:index + 1, 1])
        evolved = evolved + scaled(weight, solution)[0]
    return evolved
```

```python
import functools

import jax
import jax.numpy as jnp
from jax import lax
from jax.experimental import pallas as pl
from jax.experimental.pallas import tpu as pltpu
from jax.sharding import PartitionSpec as P

COUPLING = 0.5
TIME_STEP = 0.25
SIGMA = 3.0
HALO = 3
K = -0.5 / 30.0
DIAGONAL = -128.0 * K - SIGMA
MOMENTS = 6
SHIFT_LANE, WEIGHT_LANE = 16, 48
VMEM = pl.BlockSpec(memory_space=pltpu.VMEM)
SMEM = pl.BlockSpec(memory_space=pltpu.SMEM)


def lanes(shape):
    return lax.broadcasted_iota(jnp.int32, shape, len(shape) - 1)


def pack_kernel(psi_ref, trap_ref, packed_ref):
    depth = psi_ref.shape[2]
    group = lanes((depth, 128)) // 8
    for half in range(2):
        packs = [jnp.zeros((depth, 128), jnp.float32)] * 3
        for g in range(16):
            row = half * 16 + g
            re, im = psi_ref[0, row], psi_ref[1, row]
            diag = trap_ref[row] + COUPLING * (re * re + im * im) + DIAGONAL
            for f, field in enumerate((re, im, diag)):
                moved = pltpu.roll(field, (8 * g + HALO) % 128, 1)
                packs[f] = jnp.where(group == g, moved, packs[f])
        for f in range(3):
            packed_ref[f, half] = packs[f]


def merged(where_ref, y1_ref, y2_ref, f, half):
    odd = lax.rem(where_ref[1], 2)
    left = (lanes(y1_ref.shape[2:]) % 8 < HALO).astype(jnp.int32)
    return jnp.where(left == odd, y1_ref[f, half], y2_ref[f, half])


def spread(pack, g):
    return pltpu.roll(pack, (128 - HALO - 8 * g) % 128, 1)


def edge_kernel(where_ref, psi_ref, trap_ref, y1_ref, y2_ref, s1_ref, s2_ref):
    rows = psi_ref.shape[1]
    even = lax.rem(where_ref[0], 2) == 0
    for f in range(3):
        for i in range(HALO):
            ends = []
            for row in (i, rows - HALO + i):
                re, im = psi_ref[0, row], psi_ref[1, row]
                own = (re, im, trap_ref[row] + COUPLING * (re * re + im * im) + DIAGONAL)[f]
                side = spread(merged(where_ref, y1_ref, y2_ref, f, row // 16), row % 16)
                ends.append(jnp.concatenate([own, side], axis=1))
            s1_ref[f, i] = jnp.where(even, ends[1], ends[0])
            s2_ref[f, i] = jnp.where(even, ends[0], ends[1])


def neighbours_z(b, first, last):
    depth = b.shape[0]
    return jnp.where(first, 0.0, pltpu.roll(b, 1, 0)) + jnp.where(last, 0.0, pltpu.roll(b, depth - 1, 0))


def products(a, b):
    return a[0] * b[0] - a[1] * b[1], a[0] * b[1] + a[1] * b[0]


def apply_kernel(
    where_ref, shift_ref, weight_ref, psi_ref, trap_ref, y1_ref, y2_ref, x1_ref, x2_ref,
    u1_ref, u2_ref, out_ref, field, first_power, second_power,
):
    rows, depth = psi_ref.shape[1:3]
    tile, pole = where_ref[0], where_ref[1]
    tiles, poles = where_ref[2], where_ref[3]
    even = lax.rem(tile, 2) == 0
    for half in range(2):
        packs = [merged(where_ref, y1_ref, y2_ref, f, half) for f in range(3)]
        for g in range(16):
            row = half * 16 + g
            re, im = psi_ref[0, row], psi_ref[1, row]
            diag = trap_ref[row] + COUPLING * (re * re + im * im) + DIAGONAL
            for f, own in enumerate((re, im, diag)):
                field[f, HALO + row, :, 0:128] = own
                field[f, HALO + row, :, 128:256] = spread(packs[f], g)
    for f in range(3):
        for i in range(HALO):
            x1, x2 = x1_ref[f, i], x2_ref[f, i]
            field[f, i] = jnp.where(even, x2, x1)
            field[f, HALO + rows + i] = jnp.where(even, x1, x2)

    z = lax.broadcasted_iota(jnp.int32, (depth, 256), 0)
    first, last = z == 0, z == depth - 1
    lane = lanes((depth, 128))
    inside = jnp.where(lane < 64, (pole < poles - 1).astype(jnp.float32), (pole > 0).astype(jnp.float32))

    def image(source, x):
        diag = field[2, x]
        result = []
        for c in range(2):
            v = source[c, x]
            s = source[c, x - 1] + source[c, x + 1]
            p = (3.0 * K) * v + K * s
            e = 3.0 * p + (5.0 * K) * v
            w = e + neighbours_z(p, first, last)
            flat = diag * v + (14.0 * K) * s + neighbours_z(e, first, last)
            total = flat + pltpu.roll(w, 1, 1) + pltpu.roll(w, 255, 1)
            result.append(jnp.concatenate([total[:, :128], total[:, 128:] * inside], axis=1))
        return result

    def fold(a):
        return a[0:8] + a[8:16]

    def sweep(source, target, reach):
        for start, there in ((HALO - reach, tile > 0), (HALO + rows, tile < tiles - 1)):
            keep = there.astype(jnp.float32)
            for i in range(reach):
                for c, value in enumerate(image(source, start + i)):
                    target[c, start + i] = value * keep

        def step(i, sums):
            x = HALO + i
            new = image(source, x)
            if target is not None:
                for c in range(2):
                    target[c, x] = new[c]
            old = [source[c, x, :, 0:128] for c in range(2)]
            new = [a[:, 0:128] for a in new]
            forms = products(old, old) + products(old, new)
            return tuple(a + fold(b) for a, b in zip(sums, forms))

        zero = jnp.zeros((8, 128), jnp.float32)
        return lax.fori_loop(0, rows, step, (zero,) * 4, unroll=2)

    sums = sweep(field, first_power, 2)
    sums += sweep(first_power, second_power, 1)
    sums += sweep(second_power, None, 0)
    for c in range(2):
        u1_ref[c] = first_power[c, HALO:HALO + rows, :, 0:128]
        u2_ref[c] = second_power[c, HALO:HALO + rows, :, 0:128]

    at = lanes((1, 128))
    line = jnp.zeros((1, 128), jnp.float32)
    for j, part in enumerate(sums):
        line = jnp.where(at == j, jnp.sum(part, keepdims=True), line)
    mine = shift_ref.shape[0]
    for i in range(mine):
        for c in range(2):
            for base, ref in ((SHIFT_LANE, shift_ref), (WEIGHT_LANE, weight_ref)):
                here = (at == base + 16 * c + mine * pole + i) & (tile == 0)
                line = jnp.where(here, ref[i, c], line)
    out_ref[...] = jnp.broadcast_to(line, out_ref.shape)


def mul(a, b):
    return a[0] * b[0] - a[1] * b[1], a[0] * b[1] + a[1] * b[0]


def add(a, b):
    return a[0] + b[0], a[1] + b[1]


def sub(a, b):
    return a[0] - b[0], a[1] - b[1]


def div(a, b):
    size = jnp.maximum(jnp.abs(b[0]), jnp.abs(b[1]))
    inverse = jnp.where(size > 0.0, 1.0 / size, 0.0)
    b = (b[0] * inverse, b[1] * inverse)
    norm = b[0] * b[0] + b[1] * b[1]
    factor = jnp.where(size > 0.0, inverse / norm, 0.0)
    return (a[0] * b[0] + a[1] * b[1]) * factor, (a[1] * b[0] - a[0] * b[1]) * factor


def coefficients(line, poles):
    at = lanes((1, 128))

    def spot(j):
        return jnp.sum(jnp.where(at == j, line, 0.0), axis=1, keepdims=True) + jnp.zeros((1, 128), jnp.float32)

    m = [(spot(2 * j), spot(2 * j + 1)) for j in range(MOMENTS)]
    shift = tuple(pltpu.roll(line, (128 - SHIFT_LANE - 16 * c) % 128, 1) for c in range(2))
    weight = tuple(pltpu.roll(line, (128 - WEIGHT_LANE - 16 * c) % 128, 1) for c in range(2))
    mean = div(m[1], m[0])
    rest = list(m)
    for level in range(1, MOMENTS):
        for j in range(MOMENTS - 1, level - 1, -1):
            rest[j] = sub(rest[j], mul(mean, rest[j - 1]))
    c0, c2, c3, c4, c5 = rest[0], rest[2], rest[3], rest[4], rest[5]
    b1, e1 = div(c2, c0), div(c3, c2)
    d2 = sub(sub(c4, mul(e1, c3)), mul(b1, c2))
    b2 = div(d2, c2)
    e2 = div(sub(sub(sub(c5, mul(e1, c4)), mul(b1, c3)), mul(e1, d2)), d2)
    base = add((shift[1] / TIME_STEP + SIGMA, -shift[0] / TIME_STEP), mean)
    g2 = add(base, e2)
    g1 = sub(add(base, e1), div(b2, g2))
    y0 = div((jnp.zeros_like(line), jnp.full_like(line, -1.0 / TIME_STEP)), sub(base, div(b1, g1)))
    y1 = div((-y0[0], -y0[1]), g1)
    y2 = div((-y1[0], -y1[1]), g2)
    k1 = sub(y1, mul(e1, y2))
    k0 = sub(y0, mul(b1, y2))
    k0 = add(sub(k0, mul(mean, k1)), mul(mul(mean, mean), y2))
    twice = mul(mean, y2)
    k1 = sub(k1, (2.0 * twice[0], 2.0 * twice[1]))
    found = []
    for k in (k0, k1, y2):
        term = mul(weight, k)
        found.append(tuple(jnp.sum(jnp.where(at < poles, part, 0.0), axis=1, keepdims=True) for part in term))
    return found


def combine_kernel(poles, psi_ref, u1_ref, u2_ref, sums_ref, out_ref):
    line = jnp.sum(sums_ref[...], axis=0, keepdims=True)
    k = coefficients(line, poles)
    rows = psi_ref.shape[1]
    k = [tuple(jnp.broadcast_to(part, (8, 128)) for part in pair) for pair in k]
    for i in range(rows):
        for h in range(psi_ref.shape[2] // 8):
            at = slice(8 * h, 8 * h + 8)
            total = None
            for pair, ref in zip(k, (psi_ref, u1_ref, u2_ref)):
                term = mul(pair, (ref[0, i, at], ref[1, i, at]))
                total = term if total is None else add(total, term)
            out_ref[0, i, at] = total[0]
            out_ref[1, i, at] = total[1]


def call(kernel, out_shape, specs, scratch=(), flops=0, bytes_accessed=0):
    return pl.pallas_call(
        kernel,
        out_shape=out_shape,
        in_specs=specs,
        out_specs=jax.tree.map(lambda _: VMEM, out_shape),
        scratch_shapes=list(scratch),
        compiler_params=pltpu.CompilerParams(vmem_limit_bytes=40 * 2**20),
        cost_estimate=pl.CostEstimate(flops=flops, bytes_accessed=bytes_accessed, transcendentals=0),
    )


def on_device(psi, trap, pole_shift, pole_weight):
    tiles, poles = lax.axis_size("tile"), lax.axis_size("pole")
    rows, depth, width = trap.shape
    f32 = functools.partial(jax.ShapeDtypeStruct, dtype=jnp.float32)
    where = jnp.stack([lax.axis_index("tile"), lax.axis_index("pole"), tiles, poles]).astype(jnp.int32)

    packed = call(pack_kernel, f32((3, 2, depth, 128)), [VMEM] * 2)(psi, trap)
    pairs = [(i, i ^ 1) for i in range(poles)]
    gaps = [(i, i + 1) for i in range(1, poles - 1, 2)]
    y2 = lax.ppermute(packed, "pole", gaps + [(b, a) for a, b in gaps])
    y1 = lax.ppermute(packed, "pole", pairs)

    edge = f32((3, HALO, depth, 256))
    s1, s2 = call(edge_kernel, (edge, edge), [SMEM] + [VMEM] * 4)(where, psi, trap, y1, y2)
    pairs = [(i, i ^ 1) for i in range(tiles)]
    gaps = [(i, i + 1) for i in range(1, tiles - 1, 2)]
    x2 = lax.ppermute(s2, "tile", gaps + [(b, a) for a, b in gaps])
    x1 = lax.ppermute(s1, "tile", pairs)

    devices = tiles * poles
    grown = pltpu.VMEM((3, rows + 2 * HALO, depth, 256), jnp.float32)
    power = pltpu.VMEM((2, rows + 2 * HALO, depth, 256), jnp.float32)
    u1, u2, line = call(
        apply_kernel,
        (f32(psi.shape), f32(psi.shape), f32((devices, 128))),
        [SMEM] * 3 + [VMEM] * 6,
        [grown, power, power],
    )(where, pole_shift, pole_weight, psi, trap, y1, y2, x1, x2)

    lines = lax.all_to_all(line.reshape(devices, 1, 128), ("pole", "tile"), 0, 0, tiled=True)
    combine = functools.partial(combine_kernel, pole_shift.shape[0] * poles)
    return call(combine, f32(psi.shape), [VMEM] * 4)(psi, u1, u2, lines.reshape(devices, 128))


def solution(mesh):
    placed = (
        P(None, "tile", None, "pole"),
        P("tile", None, "pole"),
        P("pole", None),
        P("pole", None),
    )
    return jax.shard_map(
        on_device,
        mesh=mesh,
        in_specs=placed,
        out_specs=P(None, "tile", None, "pole"),
        check_vma=False,
    )
```

```python
import functools

import jax
import jax.numpy as jnp
from jax import lax
from jax.experimental import pallas as pl
from jax.experimental.pallas import tpu as pltpu
from jax.sharding import PartitionSpec as P

COUPLING = 0.5
TIME_STEP = 0.25
SIGMA = 3.0
HALO = 3
K = -0.5 / 30.0
DIAGONAL = -128.0 * K - SIGMA
MOMENTS = 6
SHIFT_LANE, WEIGHT_LANE = 16, 48
VMEM = pl.BlockSpec(memory_space=pltpu.VMEM)


def lanes(shape):
    return lax.broadcasted_iota(jnp.int32, shape, len(shape) - 1)


def position():
    return lax.axis_index("tile"), lax.axis_index("pole")


def is_odd(index):
    return lax.rem(index, 2) == 1


def load_kernel(psi_ref, trap_ref, packed_ref, field_ref, sems):
    rows, depth = trap_ref.shape[:2]
    half_rows = rows // 2
    copies = []
    for half in range(2):
        at = pl.ds(half * half_rows, half_rows)
        pair = (
            pltpu.make_async_copy(psi_ref.at[:, at], field_ref.at[0:2, at], sems.at[half, 0]),
            pltpu.make_async_copy(trap_ref.at[at], field_ref.at[2, at], sems.at[half, 1]),
        )
        for copy in pair:
            copy.start()
        copies.append(pair)
    group = lanes((depth, 128)) // 8
    for half in range(2):
        for copy in copies[half]:
            copy.wait()
        packs = [jnp.zeros((depth, 128), jnp.float32)] * 3
        for g in range(half_rows):
            row = half * half_rows + g
            re, im = field_ref[0, row], field_ref[1, row]
            diag = field_ref[2, row] + COUPLING * (re * re + im * im) + DIAGONAL
            field_ref[2, row] = diag
            for f, field in enumerate((re, im, diag)):
                moved = pltpu.roll(field, (8 * g + HALO) % 128, 1)
                packs[f] = jnp.where(group == g, moved, packs[f])
        for f in range(3):
            packed_ref[f, half] = packs[f]


def merged(y1_ref, y2_ref, f, half):
    odd = is_odd(position()[1]).astype(jnp.int32)
    left = (lanes(y1_ref.shape[2:]) % 8 < HALO).astype(jnp.int32)
    return jnp.where(left == odd, y1_ref[f, half], y2_ref[f, half])


def spread(pack, g):
    return pltpu.roll(pack, (128 - HALO - 8 * g) % 128, 1)


def edge_items(rows, high):
    start = rows - HALO if high else 0
    skip = 1 if high else 0
    return [(f, start + i) for f in range(2) for i in range(HALO)] + [(2, start + skip + i) for i in range(HALO - 1)]


def edge_kernel(field_ref, y1_ref, y2_ref, s1_ref, s2_ref):
    rows, depth = field_ref.shape[1:3]
    even = jnp.logical_not(is_odd(position()[0]))
    group = lanes((depth, 128)) // 8
    ends = []
    for high in (False, True):
        items = edge_items(rows, high)
        sides = jnp.zeros((depth, 128), jnp.float32)
        for f, first in ((0, 0), (1, HALO), (2, 2 * HALO)):
            row = items[first][1]
            pack = merged(y1_ref, y2_ref, f, row // 16)
            moved = pltpu.roll(pack, (8 * (first - row)) % 128, 1)
            sides = jnp.where(group >= first, moved, sides)
        ends.append([field_ref[f, row] for f, row in items] + [sides])
    for i, (low, high) in enumerate(zip(*ends)):
        s1_ref[i] = jnp.where(even, high, low)
        s2_ref[i] = jnp.where(even, low, high)


def neighbours_z(b):
    depth = b.shape[0]
    z = lax.broadcasted_iota(jnp.int32, b.shape, 0)
    below = jnp.where(z == 0, 0.0, pltpu.roll(b, 1, 0))
    return below + jnp.where(z == depth - 1, 0.0, pltpu.roll(b, depth - 1, 0))


def inside_mask(depth):
    pole, poles = position()[1], lax.axis_size("pole")
    lane = lanes((depth, 128))
    return jnp.where(lane < 64, (pole < poles - 1).astype(jnp.float32), (pole > 0).astype(jnp.float32))


def image(before, v, after, diag, inside):
    s = before + after
    p = (3.0 * K) * v + K * s
    e = 3.0 * p + (5.0 * K) * v
    w = e + neighbours_z(p)
    flat = diag * v + (14.0 * K) * s + neighbours_z(e)
    total = flat + pltpu.roll(w, 1, 1) + pltpu.roll(w, 255, 1)
    return jnp.concatenate([total[:, :128], total[:, 128:] * inside], axis=1)


def fold(a):
    return a[0:8, 0:128] + a[8:16, 0:128]


def forms(a, b):
    return fold(a[0] * b[0] - a[1] * b[1]), fold(a[0] * b[1] + a[1] * b[0])


def inner_kernel(field_ref, y1_ref, y2_ref, grown_ref, u1_ref, u2_ref, sums_ref):
    rows, depth = field_ref.shape[1:3]
    for half in range(2):
        packs = [merged(y1_ref, y2_ref, f, half) for f in range(3)]
        for g in range(16):
            row = half * 16 + g
            for f in range(3):
                grown_ref[f, row, :, 0:128] = field_ref[f, row]
                grown_ref[f, row, :, 128:256] = spread(packs[f], g)
    inside = inside_mask(depth)

    def sweep(source, target, reach):
        def step(i, sums):
            x = reach + i
            old = [source[c, x] for c in range(2)]
            new = [image(source[c, x - 1], old[c], source[c, x + 1], grown_ref[2, x], inside) for c in range(2)]
            if target is not None:
                for c in range(2):
                    target[c, x] = new[c]
            return tuple(a + b for a, b in zip(sums, forms(old, old) + forms(old, new)))

        zero = jnp.zeros((8, 128), jnp.float32)
        return lax.fori_loop(0, rows - 2 * reach, step, (zero,) * 4, unroll=2)

    sums = sweep(grown_ref, u1_ref, 1) + sweep(u1_ref, u2_ref, 2) + sweep(u2_ref, None, 3)
    for j, part in enumerate(sums):
        sums_ref[j] = part


def outer_kernel(
    shift_ref, weight_ref, grown_ref, u1_ref, u2_ref, sums_ref, x1_ref, x2_ref, b1_ref, b2_ref, line_ref,
):
    rows, depth = grown_ref.shape[1:3]
    tile, pole = position()
    tiles = lax.axis_size("tile")
    even = jnp.logical_not(is_odd(tile))
    inside = inside_mask(depth)
    sums = [sums_ref[j] for j in range(2 * MOMENTS)]

    def count(j, parts):
        for i, part in enumerate(parts):
            sums[j + i] += part

    for high in (False, True):
        own = (lambda i: rows - 1 + HALO - i) if high else (lambda i: i - HALO)
        there = (tile < tiles - 1) if high else (tile > 0)
        keep = jnp.where(there, inside, 0.0)
        keep = jnp.concatenate([jnp.broadcast_to(there.astype(jnp.float32), inside.shape), keep], axis=1)
        ones = jnp.concatenate([jnp.ones_like(inside), inside], axis=1)
        near, far = (x1_ref, x2_ref) if high else (x2_ref, x1_ref)
        sides = jnp.where(even, near[8], far[8])
        v, diag = [{}, {}], {}
        for item, (f, row) in enumerate(edge_items(rows, not high)):
            value = jnp.concatenate([jnp.where(even, near[item], far[item]), spread(sides, item)], axis=1)
            place = HALO - 1 - row if high else row - (rows - HALO)
            if f < 2:
                v[f][place] = value
            else:
                diag[place] = value
        for i in range(HALO, 2 * HALO):
            for c in range(2):
                v[c][i] = grown_ref[c, own(i)]
            diag[i] = grown_ref[2, own(i)]

        def powers(source, first, last):
            return [
                {
                    i: image(source[c][i - 1], source[c][i], source[c][i + 1], diag[i], inside)
                    for i in range(first, last)
                }
                for c in range(2)
            ]

        def cut(found):
            for c in range(2):
                for i in found[c]:
                    if i < HALO:
                        found[c][i] = found[c][i] * keep
            return found

        def at(source, i):
            return [source[c][i] for c in range(2)]

        u1 = cut(powers(v, 1, HALO + 1))
        for c in range(2):
            for i in range(HALO + 1, HALO + 3):
                u1[c][i] = u1_ref[c, own(i)]
        u2 = cut(powers(u1, 2, HALO + 2))
        for c in range(2):
            for i in range(HALO + 2, HALO + 4):
                u2[c][i] = u2_ref[c, own(i)]
        u3 = powers(u2, HALO, HALO + 3)

        count(0, forms(at(v, HALO), at(v, HALO)))
        count(2, forms(at(v, HALO), at(u1, HALO)))
        for i in range(HALO, HALO + 2):
            count(4, forms(at(u1, i), at(u1, i)))
            count(6, forms(at(u1, i), at(u2, i)))
        for i in range(HALO, HALO + 3):
            count(8, forms(at(u2, i), at(u2, i)))
            count(10, forms(at(u2, i), at(u3, i)))
        for c in range(2):
            b1_ref[c, 1 if high else 0] = u1[c][HALO][:, 0:128]
            for i in range(2):
                b2_ref[c, 3 - i if high else i] = u2[c][HALO + i][:, 0:128]

    lane = lanes((1, 128))
    line = jnp.zeros((1, 128), jnp.float32)
    for j, part in enumerate(sums):
        line = jnp.where(lane == j, jnp.sum(part, keepdims=True), line)
    mine = shift_ref.shape[0]
    for i in range(mine):
        for c in range(2):
            for base, ref in ((SHIFT_LANE, shift_ref), (WEIGHT_LANE, weight_ref)):
                here = (lane == base + 16 * c + mine * pole + i) & (tile == 0)
                line = jnp.where(here, ref[i:i + 1, c:c + 1], line)
    line_ref[...] = jnp.broadcast_to(line, line_ref.shape)


def mul(a, b):
    return a[0] * b[0] - a[1] * b[1], a[0] * b[1] + a[1] * b[0]


def add(a, b):
    return a[0] + b[0], a[1] + b[1]


def sub(a, b):
    return a[0] - b[0], a[1] - b[1]


def div(a, b):
    size = jnp.maximum(jnp.abs(b[0]), jnp.abs(b[1]))
    inverse = jnp.where(size > 0.0, 1.0 / size, 0.0)
    b = (b[0] * inverse, b[1] * inverse)
    norm = b[0] * b[0] + b[1] * b[1]
    factor = jnp.where(size > 0.0, inverse / norm, 0.0)
    return (a[0] * b[0] + a[1] * b[1]) * factor, (a[1] * b[0] - a[0] * b[1]) * factor


def coefficients(line, poles):
    at = lanes((1, 128))

    def spot(j):
        return jnp.sum(jnp.where(at == j, line, 0.0), axis=1, keepdims=True) + jnp.zeros((1, 128), jnp.float32)

    m = [(spot(2 * j), spot(2 * j + 1)) for j in range(MOMENTS)]
    shift = tuple(pltpu.roll(line, (128 - SHIFT_LANE - 16 * c) % 128, 1) for c in range(2))
    weight = tuple(pltpu.roll(line, (128 - WEIGHT_LANE - 16 * c) % 128, 1) for c in range(2))
    mean = div(m[1], m[0])
    rest = list(m)
    for level in range(1, MOMENTS):
        for j in range(MOMENTS - 1, level - 1, -1):
            rest[j] = sub(rest[j], mul(mean, rest[j - 1]))
    c0, c2, c3, c4, c5 = rest[0], rest[2], rest[3], rest[4], rest[5]
    b1, e1 = div(c2, c0), div(c3, c2)
    d2 = sub(sub(c4, mul(e1, c3)), mul(b1, c2))
    b2 = div(d2, c2)
    e2 = div(sub(sub(sub(c5, mul(e1, c4)), mul(b1, c3)), mul(e1, d2)), d2)
    base = add((shift[1] / TIME_STEP + SIGMA, -shift[0] / TIME_STEP), mean)
    g2 = add(base, e2)
    g1 = sub(add(base, e1), div(b2, g2))
    y0 = div((jnp.zeros_like(line), jnp.full_like(line, -1.0 / TIME_STEP)), sub(base, div(b1, g1)))
    y1 = div((-y0[0], -y0[1]), g1)
    y2 = div((-y1[0], -y1[1]), g2)
    k1 = sub(y1, mul(e1, y2))
    k0 = sub(y0, mul(b1, y2))
    k0 = add(sub(k0, mul(mean, k1)), mul(mul(mean, mean), y2))
    twice = mul(mean, y2)
    k1 = sub(k1, (2.0 * twice[0], 2.0 * twice[1]))
    found = []
    for k in (k0, k1, y2):
        term = mul(weight, k)
        found.append(tuple(jnp.sum(jnp.where(at < poles, part, 0.0), axis=1, keepdims=True) for part in term))
    return found


def combine_kernel(poles, field_ref, u1_ref, u2_ref, b1_ref, b2_ref, sums_ref, out_ref):
    line = jnp.sum(sums_ref[...], axis=0, keepdims=True)
    k = coefficients(line, poles)
    rows = field_ref.shape[1]
    k = [tuple(jnp.broadcast_to(part, (8, 128)) for part in pair) for pair in k]

    def source(inner, outer, reach, i):
        if i < reach:
            return outer, i
        if i >= rows - reach:
            return outer, i - rows + 2 * reach
        return inner, i

    for i in range(rows):
        places = ((field_ref, i), source(u1_ref, b1_ref, 1, i), source(u2_ref, b2_ref, 2, i))
        for h in range(field_ref.shape[2] // 8):
            at = slice(8 * h, 8 * h + 8)
            total = None
            for pair, (ref, x) in zip(k, places):
                term = mul(pair, (ref[0, x, at, 0:128], ref[1, x, at, 0:128]))
                total = term if total is None else add(total, term)
            out_ref[0, i, at] = total[0]
            out_ref[1, i, at] = total[1]


def call(kernel, out_shape, specs, scratch=(), flops=0, bytes_accessed=0):
    return pl.pallas_call(
        kernel,
        out_shape=out_shape,
        in_specs=specs,
        out_specs=jax.tree.map(lambda _: VMEM, out_shape),
        scratch_shapes=list(scratch),
        compiler_params=pltpu.CompilerParams(vmem_limit_bytes=32 * 2**20),
        cost_estimate=pl.CostEstimate(flops=flops, bytes_accessed=bytes_accessed, transcendentals=0),
    )


def swaps(axis):
    size = lax.axis_size(axis)
    gaps = [(i, i + 1) for i in range(1, size - 1, 2)]
    return [(i, i ^ 1) for i in range(size)], gaps + [(b, a) for a, b in gaps]


def on_device(psi, trap, pole_shift, pole_weight):
    tiles, poles = lax.axis_size("tile"), lax.axis_size("pole")
    rows, depth, width = trap.shape
    f32 = functools.partial(jax.ShapeDtypeStruct, dtype=jnp.float32)
    anywhere = pl.BlockSpec(memory_space=pl.ANY)

    packed, field = call(
        load_kernel, (f32((3, 2, depth, 128)), f32((3, rows, depth, width))), [anywhere] * 2,
        [pltpu.SemaphoreType.DMA((2, 2))],
    )(psi, trap)
    near, across = swaps("pole")
    y2 = lax.ppermute(packed, "pole", across)
    y1 = lax.ppermute(packed, "pole", near)

    edge = f32((3 * HALO, depth, 128))
    s1, s2 = call(edge_kernel, (edge, edge), [VMEM] * 3)(field, y1, y2)
    near, across = swaps("tile")
    x2 = lax.ppermute(s2, "tile", across)
    x1 = lax.ppermute(s1, "tile", near)

    wide = f32((2, rows, depth, 2 * width))
    grown, u1, u2, sums = call(
        inner_kernel,
        (f32((3, rows, depth, 2 * width)), wide, wide, f32((2 * MOMENTS, 8, 128))),
        [VMEM] * 3, flops=20_000_000, bytes_accessed=8_000_000,
    )(field, y1, y2)
    devices = tiles * poles
    b1, b2, line = call(
        outer_kernel,
        (f32((2, 2, depth, width)), f32((2, 4, depth, width)), f32((devices, 128))),
        [VMEM] * 8,
    )(pole_shift, pole_weight, grown, u1, u2, sums, x1, x2)

    lines = lax.all_to_all(line.reshape(devices, 1, 128), ("pole", "tile"), 0, 0, tiled=True)
    combine = functools.partial(combine_kernel, pole_shift.shape[0] * poles)
    return call(combine, f32(psi.shape), [VMEM] * 6)(field, u1, u2, b1, b2, lines.reshape(devices, 128))


def solution(mesh):
    placed = (
        P(None, "tile", None, "pole"),
        P("tile", None, "pole"),
        P("pole", None),
        P("pole", None),
    )
    return jax.shard_map(
        on_device,
        mesh=mesh,
        in_specs=placed,
        out_specs=P(None, "tile", None, "pole"),
        check_vma=False,
    )
```

```python
import functools

import jax
import jax.numpy as jnp
from jax import lax
from jax.experimental import pallas as pl
from jax.experimental.pallas import tpu as pltpu
from jax.sharding import PartitionSpec as P

COUPLING = 0.5
TIME_STEP = 0.25
SIGMA = 3.0
HALO = 3
K = -0.5 / 30.0
DIAGONAL = -128.0 * K - SIGMA
MOMENTS = 6
SHIFT_LANE, WEIGHT_LANE = 16, 48
VMEM = pl.BlockSpec(memory_space=pltpu.VMEM)
ANYWHERE = pl.BlockSpec(memory_space=pl.ANY)


def lanes(shape):
    return lax.broadcasted_iota(jnp.int32, shape, len(shape) - 1)


def position():
    return lax.axis_index("tile"), lax.axis_index("pole")


def is_odd(index):
    return lax.rem(index, 2) == 1


def load_kernel(psi_ref, trap_ref, packed_ref, field_ref, sems):
    rows, depth = trap_ref.shape[:2]
    half_rows = rows // 2
    copies = (
        pltpu.make_async_copy(psi_ref, field_ref.at[0:2], sems.at[0]),
        pltpu.make_async_copy(trap_ref, field_ref.at[2], sems.at[1]),
    )
    for copy in copies:
        copy.start()
    for copy in copies:
        copy.wait()
    group = lanes((depth, 128)) // 8
    for half in range(2):
        packs = [jnp.zeros((depth, 128), jnp.float32)] * 3
        for g in range(half_rows):
            row = half * half_rows + g
            re, im = field_ref[0, row], field_ref[1, row]
            diag = field_ref[2, row] + COUPLING * (re * re + im * im) + DIAGONAL
            field_ref[2, row] = diag
            for f, field in enumerate((re, im, diag)):
                moved = pltpu.roll(field, (8 * g + HALO) % 128, 1)
                packs[f] = jnp.where(group == g, moved, packs[f])
        for f in range(3):
            packed_ref[f, half] = packs[f]


def merged(y1_ref, y2_ref, f, half):
    odd = is_odd(position()[1]).astype(jnp.int32)
    left = (lanes(y1_ref.shape[2:]) % 8 < HALO).astype(jnp.int32)
    return jnp.where(left == odd, y1_ref[f, half], y2_ref[f, half])


def spread(pack, g):
    return pltpu.roll(pack, (128 - HALO - 8 * g) % 128, 1)


def edge_items(rows, high):
    start = rows - HALO if high else 0
    skip = 1 if high else 0
    return [(f, start + i) for f in range(2) for i in range(HALO)] + [(2, start + skip + i) for i in range(HALO - 1)]


def edge_kernel(field_ref, y1_ref, y2_ref, s1_ref, s2_ref):
    rows, depth = field_ref.shape[1:3]
    even = jnp.logical_not(is_odd(position()[0]))
    group = lanes((depth, 128)) // 8
    ends = []
    for high in (False, True):
        items = edge_items(rows, high)
        sides = jnp.zeros((depth, 128), jnp.float32)
        for f, first in ((0, 0), (1, HALO), (2, 2 * HALO)):
            row = items[first][1]
            pack = merged(y1_ref, y2_ref, f, row // 16)
            moved = pltpu.roll(pack, (8 * (first - row)) % 128, 1)
            sides = jnp.where(group >= first, moved, sides)
        ends.append([field_ref[f, row] for f, row in items] + [sides])
    for i, (low, high) in enumerate(zip(*ends)):
        s1_ref[i] = jnp.where(even, high, low)
        s2_ref[i] = jnp.where(even, low, high)


def neighbours_z(b):
    z = lax.broadcasted_iota(jnp.int32, (8, b.shape[1]), 0)
    low, high = b[0:8], b[8:16]
    low_up, high_up = pltpu.roll(low, 1, 0), pltpu.roll(high, 1, 0)
    low_down, high_down = pltpu.roll(low, 7, 0), pltpu.roll(high, 7, 0)
    return jnp.concatenate(
        [
            jnp.where(z == 0, 0.0, low_up) + jnp.where(z == 7, high_down, low_down),
            jnp.where(z == 0, low_up, high_up) + jnp.where(z == 7, 0.0, high_down),
        ],
        axis=0,
    )


def inside_mask(depth):
    pole, poles = position()[1], lax.axis_size("pole")
    lane = lanes((depth, 128))
    return jnp.where(lane < 64, (pole < poles - 1).astype(jnp.float32), (pole > 0).astype(jnp.float32))


def image(before, v, after, diag, inside):
    s = before + after
    p = (3.0 * K) * v + K * s
    e = 3.0 * p + (5.0 * K) * v
    w = e + neighbours_z(p)
    flat = diag * v + (14.0 * K) * s + neighbours_z(e)
    total = flat + pltpu.roll(w, 1, 1) + pltpu.roll(w, 255, 1)
    return jnp.concatenate([total[:, :128], total[:, 128:] * inside], axis=1)


def fold(a):
    return a[0:8, 0:128] + a[8:16, 0:128]


def forms(a, b):
    return fold(a[0] * b[0] - a[1] * b[1]), fold(a[0] * b[1] + a[1] * b[0])


def inner_kernel(field_ref, y1_ref, y2_ref, grown_ref, u1_ref, u2_ref, sums_ref):
    rows, depth = field_ref.shape[1:3]
    for half in range(2):
        packs = [merged(y1_ref, y2_ref, f, half) for f in range(3)]
        for g in range(16):
            row = half * 16 + g
            for f in range(3):
                grown_ref[f, row, :, 0:128] = field_ref[f, row]
                grown_ref[f, row, :, 128:256] = spread(packs[f], g)
    inside = inside_mask(depth)

    def sweep(source, target, reach):
        def step(i, sums):
            x = reach + i
            old = [source[c, x] for c in range(2)]
            new = [image(source[c, x - 1], old[c], source[c, x + 1], grown_ref[2, x], inside) for c in range(2)]
            if target is not None:
                for c in range(2):
                    target[c, x] = new[c]
            return tuple(a + b for a, b in zip(sums, forms(old, old) + forms(old, new)))

        zero = jnp.zeros((8, 128), jnp.float32)
        return lax.fori_loop(0, rows - 2 * reach, step, (zero,) * 4, unroll=True)

    sums = sweep(grown_ref, u1_ref, 1) + sweep(u1_ref, u2_ref, 2) + sweep(u2_ref, None, 3)
    for j, part in enumerate(sums):
        sums_ref[j] = part


def outer_kernel(
    shift_ref, weight_ref, grown_ref, u1_ref, u2_ref, sums_ref, x2_ref, x1_ref, b1_ref, b2_ref, line_ref,
):
    rows, depth = grown_ref.shape[1:3]
    tile, pole = position()
    tiles = lax.axis_size("tile")
    even = jnp.logical_not(is_odd(tile))
    inside = inside_mask(depth)
    sums = [sums_ref[j] for j in range(2 * MOMENTS)]

    def count(j, parts):
        for i, part in enumerate(parts):
            sums[j + i] += part

    for high in (False, True):
        own = (lambda i: rows - 1 + HALO - i) if high else (lambda i: i - HALO)
        there = (tile < tiles - 1) if high else (tile > 0)
        keep = jnp.where(there, inside, 0.0)
        keep = jnp.concatenate([jnp.broadcast_to(there.astype(jnp.float32), inside.shape), keep], axis=1)
        ones = jnp.concatenate([jnp.ones_like(inside), inside], axis=1)
        near, far = (x1_ref, x2_ref) if high else (x2_ref, x1_ref)
        sides = jnp.where(even, near[8], far[8])
        v, diag = [{}, {}], {}
        for item, (f, row) in enumerate(edge_items(rows, not high)):
            value = jnp.concatenate([jnp.where(even, near[item], far[item]), spread(sides, item)], axis=1)
            place = HALO - 1 - row if high else row - (rows - HALO)
            if f < 2:
                v[f][place] = value
            else:
                diag[place] = value
        for i in range(HALO, 2 * HALO):
            for c in range(2):
                v[c][i] = grown_ref[c, own(i)]
            diag[i] = grown_ref[2, own(i)]

        def powers(source, first, last):
            return [
                {
                    i: image(source[c][i - 1], source[c][i], source[c][i + 1], diag[i], inside)
                    for i in range(first, last)
                }
                for c in range(2)
            ]

        def cut(found):
            for c in range(2):
                for i in found[c]:
                    if i < HALO:
                        found[c][i] = found[c][i] * keep
            return found

        def at(source, i):
            return [source[c][i] for c in range(2)]

        u1 = cut(powers(v, 1, HALO + 1))
        for c in range(2):
            for i in range(HALO + 1, HALO + 3):
                u1[c][i] = u1_ref[c, own(i)]
        u2 = cut(powers(u1, 2, HALO + 2))
        for c in range(2):
            for i in range(HALO + 2, HALO + 4):
                u2[c][i] = u2_ref[c, own(i)]
        u3 = powers(u2, HALO, HALO + 3)

        count(0, forms(at(v, HALO), at(v, HALO)))
        count(2, forms(at(v, HALO), at(u1, HALO)))
        for i in range(HALO, HALO + 2):
            count(4, forms(at(u1, i), at(u1, i)))
            count(6, forms(at(u1, i), at(u2, i)))
        for i in range(HALO, HALO + 3):
            count(8, forms(at(u2, i), at(u2, i)))
            count(10, forms(at(u2, i), at(u3, i)))
        for c in range(2):
            b1_ref[c, 1 if high else 0] = u1[c][HALO][:, 0:128]
            for i in range(2):
                b2_ref[c, 3 - i if high else i] = u2[c][HALO + i][:, 0:128]

    lane = lanes((1, 128))
    line = jnp.zeros((1, 128), jnp.float32)
    for j, part in enumerate(sums):
        line = jnp.where(lane == j, jnp.sum(part, keepdims=True), line)
    mine = shift_ref.shape[0]
    for i in range(mine):
        for c in range(2):
            for base, ref in ((SHIFT_LANE, shift_ref), (WEIGHT_LANE, weight_ref)):
                here = (lane == base + 16 * c + mine * pole + i) & (tile == 0)
                line = jnp.where(here, ref[i:i + 1, c:c + 1], line)
    line_ref[...] = jnp.broadcast_to(line, line_ref.shape)


def mul(a, b):
    return a[0] * b[0] - a[1] * b[1], a[0] * b[1] + a[1] * b[0]


def add(a, b):
    return a[0] + b[0], a[1] + b[1]


def sub(a, b):
    return a[0] - b[0], a[1] - b[1]


def over(a, b):
    norm = b[0] * b[0] + b[1] * b[1]
    factor = jnp.where(norm > 0.0, 1.0 / norm, 0.0)
    return (a[0] * b[0] + a[1] * b[1]) * factor, (a[1] * b[0] - a[0] * b[1]) * factor


def coefficients(line, poles):
    at = lanes((1, 128))

    def spot(j):
        return jnp.sum(jnp.where(at == j, line, 0.0), axis=1, keepdims=True) + jnp.zeros((1, 128), jnp.float32)

    m = [(spot(2 * j), spot(2 * j + 1)) for j in range(MOMENTS)]
    shift = tuple(pltpu.roll(line, (128 - SHIFT_LANE - 16 * c) % 128, 1) for c in range(2))
    weight = tuple(pltpu.roll(line, (128 - WEIGHT_LANE - 16 * c) % 128, 1) for c in range(2))
    scale = 1.0 / jnp.maximum(jnp.abs(m[0][0]), jnp.abs(m[0][1]))
    m = [(re * scale, im * scale) for re, im in m]
    mean = over(m[1], m[0])
    rest = list(m)
    for level in range(1, MOMENTS):
        for j in range(MOMENTS - 1, level - 1, -1):
            rest[j] = sub(rest[j], mul(mean, rest[j - 1]))
    c0, c2, c3, c4, c5 = rest[0], rest[2], rest[3], rest[4], rest[5]
    b1, e1 = over(c2, c0), over(c3, c2)
    d2 = sub(sub(c4, mul(e1, c3)), mul(b1, c2))
    b2 = over(d2, c2)
    e2 = over(sub(sub(sub(c5, mul(e1, c4)), mul(b1, c3)), mul(e1, d2)), d2)
    base = add((shift[1] / TIME_STEP + SIGMA, -shift[0] / TIME_STEP), mean)
    g2 = add(base, e2)
    g1 = sub(mul(add(base, e1), g2), b2)
    source = over((jnp.zeros_like(line), jnp.full_like(line, -1.0 / TIME_STEP)), sub(mul(base, g1), mul(b1, g2)))
    y0, y1, y2 = mul(source, g1), mul((-source[0], -source[1]), g2), source
    k1 = sub(y1, mul(e1, y2))
    k0 = sub(y0, mul(b1, y2))
    k0 = add(sub(k0, mul(mean, k1)), mul(mul(mean, mean), y2))
    twice = mul(mean, y2)
    k1 = sub(k1, (2.0 * twice[0], 2.0 * twice[1]))
    found = []
    for k in (k0, k1, y2):
        term = mul(weight, k)
        found.append(tuple(jnp.sum(jnp.where(at < poles, part, 0.0), axis=1, keepdims=True) for part in term))
    return found


def combine_kernel(poles, field_ref, u1_ref, u2_ref, b1_ref, b2_ref, sums_ref, out_ref, held, sems):
    line = jnp.sum(sums_ref[...], axis=0, keepdims=True)
    k = coefficients(line, poles)
    rows = field_ref.shape[1]
    k = [tuple(jnp.broadcast_to(part, (8, 128)) for part in pair) for pair in k]

    def source(inner, outer, reach, i):
        if i < reach:
            return outer, i
        if i >= rows - reach:
            return outer, i - rows + 2 * reach
        return inner, i

    parts = 2
    copies = []
    for i in range(rows):
        places = ((field_ref, i), source(u1_ref, b1_ref, 1, i), source(u2_ref, b2_ref, 2, i))
        for h in range(field_ref.shape[2] // 8):
            at = slice(8 * h, 8 * h + 8)
            total = None
            for pair, (ref, x) in zip(k, places):
                term = mul(pair, (ref[0, x, at, 0:128], ref[1, x, at, 0:128]))
                total = term if total is None else add(total, term)
            held[0, i, at] = total[0]
            held[1, i, at] = total[1]
        if (i + 1) % (rows // parts) == 0:
            part = pl.ds(i + 1 - rows // parts, rows // parts)
            for c in range(2):
                copy = pltpu.make_async_copy(held.at[c, part], out_ref.at[c, part], sems.at[c, len(copies) // 2])
                copy.start()
                copies.append(copy)
    for copy in copies:
        copy.wait()


def call(kernel, out_shape, specs, scratch=(), flops=0, bytes_accessed=0, aliases={}, out_spec=VMEM):
    return pl.pallas_call(
        kernel,
        out_shape=out_shape,
        in_specs=specs,
        out_specs=jax.tree.map(lambda _: out_spec, out_shape),
        scratch_shapes=list(scratch),
        input_output_aliases=aliases,
        compiler_params=pltpu.CompilerParams(vmem_limit_bytes=32 * 2**20),
        cost_estimate=pl.CostEstimate(flops=flops, bytes_accessed=bytes_accessed, transcendentals=0),
    )


def swaps(axis):
    size = lax.axis_size(axis)
    gaps = [(i, i + 1) for i in range(1, size - 1, 2)]
    return [(i, i ^ 1) for i in range(size)], gaps + [(b, a) for a, b in gaps]


def on_device(psi, trap, pole_shift, pole_weight):
    tiles, poles = lax.axis_size("tile"), lax.axis_size("pole")
    rows, depth, width = trap.shape
    f32 = functools.partial(jax.ShapeDtypeStruct, dtype=jnp.float32)

    psi, trap = (pltpu.with_memory_space_constraint(x, pltpu.HBM) for x in (psi, trap))
    packed, field = call(
        load_kernel, (f32((3, 2, depth, 128)), f32((3, rows, depth, width))), [ANYWHERE] * 2,
        [pltpu.SemaphoreType.DMA((2,))],
    )(psi, trap)
    near, across = swaps("pole")
    y2 = lax.ppermute(packed, "pole", across)
    y1 = lax.ppermute(packed, "pole", near)

    edge = f32((3 * HALO, depth, 128))
    s1, s2 = call(edge_kernel, (edge, edge), [VMEM] * 3)(field, y1, y2)
    near, across = swaps("tile")
    x2 = lax.ppermute(s2, "tile", across)
    x1 = lax.ppermute(s1, "tile", near)

    wide = f32((2, rows, depth, 2 * width))
    grown, u1, u2, sums = call(
        inner_kernel,
        (f32((3, rows, depth, 2 * width)), wide, wide, f32((2 * MOMENTS, 8, 128))),
        [VMEM] * 3, flops=20_000_000, bytes_accessed=8_000_000,
    )(field, y1, y2)
    devices = tiles * poles
    b1, b2, line = call(
        outer_kernel,
        (f32((2, 2, depth, width)), f32((2, 4, depth, width)), f32((devices, 128))),
        [VMEM] * 8,
    )(pole_shift, pole_weight, grown, u1, u2, sums, x2, x1)

    lines = lax.all_to_all(line.reshape(devices, 1, 128), ("pole", "tile"), 0, 0, tiled=True)
    combine = functools.partial(combine_kernel, pole_shift.shape[0] * poles)
    return call(
        combine, f32((2, rows, depth, width)), [VMEM] * 6,
        [pltpu.VMEM((2, rows, depth, width), jnp.float32), pltpu.SemaphoreType.DMA((2, 2))], out_spec=ANYWHERE,
    )(field, u1, u2, b1, b2, lines.reshape(devices, 128))


def solution(mesh):
    placed = (
        P(None, "tile", None, "pole"),
        P("tile", None, "pole"),
        P("pole", None),
        P("pole", None),
    )
    return jax.shard_map(
        on_device,
        mesh=mesh,
        in_specs=placed,
        out_specs=P(None, "tile", None, "pole"),
        check_vma=False,
    )
```

```python
import functools

import jax
import jax.numpy as jnp
from jax import lax
from jax.experimental import pallas as pl
from jax.experimental.pallas import tpu as pltpu
from jax.sharding import PartitionSpec as P

COUPLING = 0.5
TIME_STEP = 0.25
SIGMA = 3.0
HALO = 3
K = -0.5 / 30.0
DIAGONAL = -128.0 * K - SIGMA
MOMENTS = 6
SHIFT_LANE, WEIGHT_LANE = 16, 48
VMEM = pl.BlockSpec(memory_space=pltpu.VMEM)
ANYWHERE = pl.BlockSpec(memory_space=pl.ANY)


def lanes(shape):
    return lax.broadcasted_iota(jnp.int32, shape, len(shape) - 1)


def position():
    return lax.axis_index("tile"), lax.axis_index("pole")


def is_odd(index):
    return lax.rem(index, 2) == 1


def load_kernel(psi_ref, trap_ref, s1_ref, s2_ref, field_ref, sems):
    rows, depth = trap_ref.shape[:2]
    half_rows, part_rows = rows // 2, rows // 2
    copies = []
    for part in range(2):
        at = pl.ds(part * part_rows, part_rows)
        pair = (
            pltpu.make_async_copy(psi_ref.at[:, at], field_ref.at[0:2, at], sems.at[part, 0]),
            pltpu.make_async_copy(trap_ref.at[at], field_ref.at[2, at], sems.at[part, 1]),
        )
        for copy in pair:
            copy.start()
        copies.append(pair)
    group = lanes((depth, 128)) // 8
    packs = [[jnp.zeros((depth, 128), jnp.float32)] * 2 for _ in range(3)]
    for row in range(rows):
        half, g = divmod(row, half_rows)
        if g == 0:
            for copy in copies[half]:
                copy.wait()
        re, im = field_ref[0, row], field_ref[1, row]
        diag = field_ref[2, row] + COUPLING * (re * re + im * im) + DIAGONAL
        field_ref[2, row] = diag
        for f, field in enumerate((re, im, diag)):
            moved = pltpu.roll(field, (8 * g + HALO) % 128, 1)
            packs[f][half] = jnp.where(group == g, moved, packs[f][half])
    first = lanes((depth, 128)) % 8 < HALO
    odd = is_odd(position()[1])
    for f in range(3):
        low, high = packs[f]
        to_right = jnp.where(first, low, pltpu.roll(high, HALO, 1))
        to_left = jnp.where(first, pltpu.roll(low, 128 - HALO, 1), high)
        s1_ref[f] = jnp.where(odd, to_left, to_right)
        s2_ref[f] = jnp.where(odd, to_right, to_left)


def merged(y1_ref, y2_ref, f, half):
    odd = is_odd(position()[1])
    first = lanes(y1_ref.shape[1:]) % 8 < HALO
    left = jnp.where(odd, y1_ref[f], y2_ref[f])
    right = jnp.where(odd, y2_ref[f], y1_ref[f])
    if half:
        return jnp.where(first, pltpu.roll(left, 128 - HALO, 1), right)
    return jnp.where(first, left, pltpu.roll(right, HALO, 1))


def spread(pack, g):
    return pltpu.roll(pack, (128 - HALO - 8 * g) % 128, 1)


def edge_items(rows, high):
    start = rows - HALO if high else 0
    skip = 1 if high else 0
    return [(f, start + i) for f in range(2) for i in range(HALO)] + [(2, start + skip + i) for i in range(HALO - 1)]


def edge_kernel(field_ref, y1_ref, y2_ref, s1_ref, s2_ref):
    rows, depth = field_ref.shape[1:3]
    even = jnp.logical_not(is_odd(position()[0]))
    group = lanes((depth, 128)) // 8
    ends = []
    for high in (False, True):
        items = edge_items(rows, high)
        sides = jnp.zeros((depth, 128), jnp.float32)
        for f, first in ((0, 0), (1, HALO), (2, 2 * HALO)):
            row = items[first][1]
            pack = merged(y1_ref, y2_ref, f, row // 16)
            moved = pltpu.roll(pack, (8 * (first - row)) % 128, 1)
            sides = jnp.where(group >= first, moved, sides)
        ends.append([field_ref[f, row] for f, row in items] + [sides])
    for i, (low, high) in enumerate(zip(*ends)):
        s1_ref[i] = jnp.where(even, high, low)
        s2_ref[i] = jnp.where(even, low, high)


def neighbours_z(b):
    z = lax.broadcasted_iota(jnp.int32, (8, b.shape[1]), 0)
    low, high = b[0:8], b[8:16]
    low_up, high_up = pltpu.roll(low, 1, 0), pltpu.roll(high, 1, 0)
    low_down, high_down = pltpu.roll(low, 7, 0), pltpu.roll(high, 7, 0)
    return jnp.concatenate(
        [
            jnp.where(z == 0, 0.0, low_up) + jnp.where(z == 7, high_down, low_down),
            jnp.where(z == 0, low_up, high_up) + jnp.where(z == 7, 0.0, high_down),
        ],
        axis=0,
    )


def inside_mask(depth):
    pole, poles = position()[1], lax.axis_size("pole")
    lane = lanes((depth, 128))
    return jnp.where(lane < 64, (pole < poles - 1).astype(jnp.float32), (pole > 0).astype(jnp.float32))


def image(before, v, after, diag, inside):
    s = before + after
    p = (3.0 * K) * v + K * s
    e = 3.0 * p + (5.0 * K) * v
    w = e + neighbours_z(p)
    flat = diag * v + (14.0 * K) * s + neighbours_z(e)
    total = flat + pltpu.roll(w, 1, 1) + pltpu.roll(w, 255, 1)
    return jnp.concatenate([total[:, :128], total[:, 128:] * inside], axis=1)


def fold(a):
    return a[0:8, 0:128] + a[8:16, 0:128]


def forms(a, b):
    return fold(a[0] * b[0] - a[1] * b[1]), fold(a[0] * b[1] + a[1] * b[0])


def inner_kernel(field_ref, y1_ref, y2_ref, grown_ref, u1_ref, u2_ref, sums_ref):
    rows, depth = field_ref.shape[1:3]
    for half in range(2):
        packs = [merged(y1_ref, y2_ref, f, half) for f in range(3)]
        for g in range(16):
            row = half * 16 + g
            for f in range(3):
                grown_ref[f, row, :, 0:128] = field_ref[f, row]
                grown_ref[f, row, :, 128:256] = spread(packs[f], g)
    inside = inside_mask(depth)

    def sweep(source, target, reach):
        def step(i, sums):
            x = reach + i
            old = [source[c, x] for c in range(2)]
            new = [image(source[c, x - 1], old[c], source[c, x + 1], grown_ref[2, x], inside) for c in range(2)]
            if target is not None:
                for c in range(2):
                    target[c, x] = new[c]
            return tuple(a + b for a, b in zip(sums, forms(old, old) + forms(old, new)))

        zero = jnp.zeros((8, 128), jnp.float32)
        return lax.fori_loop(0, rows - 2 * reach, step, (zero,) * 4, unroll=True)

    sums = sweep(grown_ref, u1_ref, 1) + sweep(u1_ref, u2_ref, 2) + sweep(u2_ref, None, 3)
    for j, part in enumerate(sums):
        sums_ref[j] = part


def outer_kernel(
    shift_ref, weight_ref, grown_ref, u1_ref, u2_ref, sums_ref, x2_ref, x1_ref, b1_ref, b2_ref, line_ref,
):
    rows, depth = grown_ref.shape[1:3]
    tile, pole = position()
    tiles = lax.axis_size("tile")
    even = jnp.logical_not(is_odd(tile))
    inside = inside_mask(depth)
    sums = [sums_ref[j] for j in range(2 * MOMENTS)]

    def count(j, parts):
        for i, part in enumerate(parts):
            sums[j + i] += part

    def end(high):
        own = (lambda i: rows - 1 + HALO - i) if high else (lambda i: i - HALO)
        there = (tile < tiles - 1) if high else (tile > 0)
        keep = jnp.where(there, inside, 0.0)
        keep = jnp.concatenate([jnp.broadcast_to(there.astype(jnp.float32), inside.shape), keep], axis=1)
        ones = jnp.concatenate([jnp.ones_like(inside), inside], axis=1)
        near, far = (x1_ref, x2_ref) if high else (x2_ref, x1_ref)
        sides = jnp.where(even, near[8], far[8])
        v, diag = [{}, {}], {}
        for item, (f, row) in enumerate(edge_items(rows, not high)):
            value = jnp.concatenate([jnp.where(even, near[item], far[item]), spread(sides, item)], axis=1)
            place = HALO - 1 - row if high else row - (rows - HALO)
            if f < 2:
                v[f][place] = value
            else:
                diag[place] = value
        for i in range(HALO, 2 * HALO):
            for c in range(2):
                v[c][i] = grown_ref[c, own(i)]
            diag[i] = grown_ref[2, own(i)]

        def powers(source, first, last):
            return [
                {
                    i: image(source[c][i - 1], source[c][i], source[c][i + 1], diag[i], inside)
                    for i in range(first, last)
                }
                for c in range(2)
            ]

        def cut(found):
            for c in range(2):
                for i in found[c]:
                    if i < HALO:
                        found[c][i] = found[c][i] * keep
            return found

        def at(source, i):
            return [source[c][i] for c in range(2)]

        yield
        u1 = cut(powers(v, 1, HALO + 1))
        yield
        for c in range(2):
            for i in range(HALO + 1, HALO + 3):
                u1[c][i] = u1_ref[c, own(i)]
        u2 = cut(powers(u1, 2, HALO + 2))
        yield
        for c in range(2):
            for i in range(HALO + 2, HALO + 4):
                u2[c][i] = u2_ref[c, own(i)]
        u3 = powers(u2, HALO, HALO + 3)
        yield

        count(0, forms(at(v, HALO), at(v, HALO)))
        count(2, forms(at(v, HALO), at(u1, HALO)))
        for i in range(HALO, HALO + 2):
            count(4, forms(at(u1, i), at(u1, i)))
            count(6, forms(at(u1, i), at(u2, i)))
        for i in range(HALO, HALO + 3):
            count(8, forms(at(u2, i), at(u2, i)))
            count(10, forms(at(u2, i), at(u3, i)))
        for c in range(2):
            b1_ref[c, 1 if high else 0] = u1[c][HALO][:, 0:128]
            for i in range(2):
                b2_ref[c, 3 - i if high else i] = u2[c][HALO + i][:, 0:128]
        yield

    for _ in zip(end(False), end(True)):
        pass

    lane = lanes((1, 128))
    line = jnp.zeros((1, 128), jnp.float32)
    for j, part in enumerate(sums):
        line = jnp.where(lane == j, jnp.sum(part, keepdims=True), line)
    mine = shift_ref.shape[0]
    for i in range(mine):
        for c in range(2):
            for base, ref in ((SHIFT_LANE, shift_ref), (WEIGHT_LANE, weight_ref)):
                here = (lane == base + 16 * c + mine * pole + i) & (tile == 0)
                line = jnp.where(here, ref[i:i + 1, c:c + 1], line)
    line_ref[...] = jnp.broadcast_to(line, line_ref.shape)


def mul(a, b):
    return a[0] * b[0] - a[1] * b[1], a[0] * b[1] + a[1] * b[0]


def add(a, b):
    return a[0] + b[0], a[1] + b[1]


def sub(a, b):
    return a[0] - b[0], a[1] - b[1]


def over(a, b):
    norm = b[0] * b[0] + b[1] * b[1]
    factor = jnp.where(norm > 0.0, 1.0 / norm, 0.0)
    return (a[0] * b[0] + a[1] * b[1]) * factor, (a[1] * b[0] - a[0] * b[1]) * factor


def coefficients(line, poles):
    at = lanes((1, 128))

    def spot(j):
        return jnp.sum(jnp.where(at == j, line, 0.0), axis=1, keepdims=True) + jnp.zeros((1, 128), jnp.float32)

    m = [(spot(2 * j), spot(2 * j + 1)) for j in range(MOMENTS)]
    shift = tuple(pltpu.roll(line, (128 - SHIFT_LANE - 16 * c) % 128, 1) for c in range(2))
    weight = tuple(pltpu.roll(line, (128 - WEIGHT_LANE - 16 * c) % 128, 1) for c in range(2))
    scale = 1.0 / jnp.maximum(jnp.abs(m[0][0]), jnp.abs(m[0][1]))
    m = [(re * scale, im * scale) for re, im in m]
    mean = over(m[1], m[0])
    rest = list(m)
    for level in range(1, MOMENTS):
        for j in range(MOMENTS - 1, level - 1, -1):
            rest[j] = sub(rest[j], mul(mean, rest[j - 1]))
    c0, c2, c3, c4, c5 = rest[0], rest[2], rest[3], rest[4], rest[5]
    b1, e1 = over(c2, c0), over(c3, c2)
    d2 = sub(sub(c4, mul(e1, c3)), mul(b1, c2))
    b2 = over(d2, c2)
    e2 = over(sub(sub(sub(c5, mul(e1, c4)), mul(b1, c3)), mul(e1, d2)), d2)
    base = add((shift[1] / TIME_STEP + SIGMA, -shift[0] / TIME_STEP), mean)
    g2 = add(base, e2)
    g1 = sub(mul(add(base, e1), g2), b2)
    source = over((jnp.zeros_like(line), jnp.full_like(line, -1.0 / TIME_STEP)), sub(mul(base, g1), mul(b1, g2)))
    y0, y1, y2 = mul(source, g1), mul((-source[0], -source[1]), g2), source
    k1 = sub(y1, mul(e1, y2))
    k0 = sub(y0, mul(b1, y2))
    k0 = add(sub(k0, mul(mean, k1)), mul(mul(mean, mean), y2))
    twice = mul(mean, y2)
    k1 = sub(k1, (2.0 * twice[0], 2.0 * twice[1]))
    found = []
    for k in (k0, k1, y2):
        term = mul(weight, k)
        found.append(tuple(jnp.sum(jnp.where(at < poles, part, 0.0), axis=1, keepdims=True) for part in term))
    return found


def combine_kernel(poles, field_ref, u1_ref, u2_ref, b1_ref, b2_ref, sums_ref, out_ref, held, sems):
    line = jnp.sum(sums_ref[...], axis=0, keepdims=True)
    k = coefficients(line, poles)
    rows = field_ref.shape[1]
    k = [tuple(jnp.broadcast_to(part, (8, 128)) for part in pair) for pair in k]

    def source(inner, outer, reach, i):
        if i < reach:
            return outer, i
        if i >= rows - reach:
            return outer, i - rows + 2 * reach
        return inner, i

    parts = 2
    copies = []
    for i in range(rows):
        places = ((field_ref, i), source(u1_ref, b1_ref, 1, i), source(u2_ref, b2_ref, 2, i))
        for h in range(field_ref.shape[2] // 8):
            at = slice(8 * h, 8 * h + 8)
            total = None
            for pair, (ref, x) in zip(k, places):
                term = mul(pair, (ref[0, x, at, 0:128], ref[1, x, at, 0:128]))
                total = term if total is None else add(total, term)
            held[0, i, at] = total[0]
            held[1, i, at] = total[1]
        if (i + 1) % (rows // parts) == 0:
            part = pl.ds(i + 1 - rows // parts, rows // parts)
            for c in range(2):
                copy = pltpu.make_async_copy(held.at[c, part], out_ref.at[c, part], sems.at[c, len(copies) // 2])
                copy.start()
                copies.append(copy)
    for copy in copies:
        copy.wait()


def call(kernel, out_shape, specs, scratch=(), flops=0, bytes_accessed=0, aliases={}, out_spec=VMEM):
    return pl.pallas_call(
        kernel,
        out_shape=out_shape,
        in_specs=specs,
        out_specs=jax.tree.map(lambda _: out_spec, out_shape),
        scratch_shapes=list(scratch),
        input_output_aliases=aliases,
        compiler_params=pltpu.CompilerParams(vmem_limit_bytes=32 * 2**20),
        cost_estimate=pl.CostEstimate(flops=flops, bytes_accessed=bytes_accessed, transcendentals=0),
    )


def swaps(axis):
    size = lax.axis_size(axis)
    gaps = [(i, i + 1) for i in range(1, size - 1, 2)]
    return [(i, i ^ 1) for i in range(size)], gaps + [(b, a) for a, b in gaps]


def on_device(psi, trap, pole_shift, pole_weight):
    tiles, poles = lax.axis_size("tile"), lax.axis_size("pole")
    rows, depth, width = trap.shape
    f32 = functools.partial(jax.ShapeDtypeStruct, dtype=jnp.float32)

    psi, trap = (pltpu.with_memory_space_constraint(x, pltpu.HBM) for x in (psi, trap))
    message = f32((3, depth, 128))
    m1, m2, field = call(
        load_kernel, (message, message, f32((3, rows, depth, width))), [ANYWHERE] * 2,
        [pltpu.SemaphoreType.DMA((2, 2))],
    )(psi, trap)
    near, across = swaps("pole")
    y2 = lax.ppermute(m2, "pole", across)
    y1 = lax.ppermute(m1, "pole", near)

    edge = f32((3 * HALO, depth, 128))
    s1, s2 = call(edge_kernel, (edge, edge), [VMEM] * 3)(field, y1, y2)
    near, across = swaps("tile")
    x2 = lax.ppermute(s2, "tile", across)
    x1 = lax.ppermute(s1, "tile", near)

    wide = f32((2, rows, depth, 2 * width))
    grown, u1, u2, sums = call(
        inner_kernel,
        (f32((3, rows, depth, 2 * width)), wide, wide, f32((2 * MOMENTS, 8, 128))),
        [VMEM] * 3, flops=20_000_000, bytes_accessed=8_000_000,
    )(field, y1, y2)
    devices = tiles * poles
    b1, b2, line = call(
        outer_kernel,
        (f32((2, 2, depth, width)), f32((2, 4, depth, width)), f32((devices, 128))),
        [VMEM] * 8,
    )(pole_shift, pole_weight, grown, u1, u2, sums, x2, x1)

    lines = lax.all_to_all(line.reshape(devices, 1, 128), ("pole", "tile"), 0, 0, tiled=True)
    combine = functools.partial(combine_kernel, pole_shift.shape[0] * poles)
    return call(
        combine, f32((2, rows, depth, width)), [VMEM] * 6,
        [pltpu.VMEM((2, rows, depth, width), jnp.float32), pltpu.SemaphoreType.DMA((2, 2))], out_spec=ANYWHERE,
    )(field, u1, u2, b1, b2, lines.reshape(devices, 128))


def solution(mesh):
    placed = (
        P(None, "tile", None, "pole"),
        P("tile", None, "pole"),
        P("pole", None),
        P("pole", None),
    )
    return jax.shard_map(
        on_device,
        mesh=mesh,
        in_specs=placed,
        out_specs=P(None, "tile", None, "pole"),
        check_vma=False,
    )
```

```python
import functools

import jax
import jax.numpy as jnp
from jax import lax
from jax.experimental import pallas as pl
from jax.experimental.pallas import tpu as pltpu
from jax.sharding import PartitionSpec as P

COUPLING = 0.5
TIME_STEP = 0.25
SIGMA = 3.0
HALO = 3
K = -0.5 / 30.0
DIAGONAL = -128.0 * K - SIGMA
MOMENTS = 6
SHIFT_LANE, WEIGHT_LANE = 16, 48
VMEM = pl.BlockSpec(memory_space=pltpu.VMEM)
ANYWHERE = pl.BlockSpec(memory_space=pl.ANY)


def lanes(shape):
    return lax.broadcasted_iota(jnp.int32, shape, len(shape) - 1)


def position():
    return lax.axis_index("tile"), lax.axis_index("pole")


def is_odd(index):
    return lax.rem(index, 2) == 1


def load_kernel(psi_ref, trap_ref, s1_ref, s2_ref, field_ref, sems):
    rows, depth = trap_ref.shape[:2]
    half_rows, part_rows = rows // 2, rows // 2
    copies = []
    for part in range(2):
        at = pl.ds(part * part_rows, part_rows)
        pair = (
            pltpu.make_async_copy(psi_ref.at[:, at], field_ref.at[0:2, at], sems.at[part, 0]),
            pltpu.make_async_copy(trap_ref.at[at], field_ref.at[2, at], sems.at[part, 1]),
        )
        for copy in pair:
            copy.start()
        copies.append(pair)
    group = lanes((depth, 128)) // 8
    packs = [[jnp.zeros((depth, 128), jnp.float32)] * 2 for _ in range(3)]
    for row in range(rows):
        half, g = divmod(row, half_rows)
        if g == 0:
            for copy in copies[half]:
                copy.wait()
        re, im = field_ref[0, row], field_ref[1, row]
        diag = field_ref[2, row] + COUPLING * (re * re + im * im) + DIAGONAL
        field_ref[2, row] = diag
        for f, field in enumerate((re, im, diag)):
            moved = pltpu.roll(field, (8 * g + HALO) % 128, 1)
            packs[f][half] = jnp.where(group == g, moved, packs[f][half])
    first = lanes((depth, 128)) % 8 < HALO
    odd = is_odd(position()[1])
    for f in range(3):
        low, high = packs[f]
        to_right = jnp.where(first, low, pltpu.roll(high, HALO, 1))
        to_left = jnp.where(first, pltpu.roll(low, 128 - HALO, 1), high)
        s1_ref[f] = jnp.where(odd, to_left, to_right)
        s2_ref[f] = jnp.where(odd, to_right, to_left)


def merged(y1_ref, y2_ref, f, half):
    odd = is_odd(position()[1])
    first = lanes(y1_ref.shape[1:]) % 8 < HALO
    pole, poles = position()[1], lax.axis_size("pole")
    left = jnp.where(odd, y1_ref[f], y2_ref[f]) * (pole > 0).astype(jnp.float32)
    right = jnp.where(odd, y2_ref[f], y1_ref[f]) * (pole < poles - 1).astype(jnp.float32)
    if half:
        return jnp.where(first, pltpu.roll(left, 128 - HALO, 1), right)
    return jnp.where(first, left, pltpu.roll(right, HALO, 1))


def spread(pack, g):
    return pltpu.roll(pack, (128 - HALO - 8 * g) % 128, 1)


def edge_items(rows, high):
    start = rows - HALO if high else 0
    skip = 1 if high else 0
    return [(f, start + i) for f in range(2) for i in range(HALO)] + [(2, start + skip + i) for i in range(HALO - 1)]


def edge_kernel(field_ref, y1_ref, y2_ref, s1_ref, s2_ref):
    rows, depth = field_ref.shape[1:3]
    even = jnp.logical_not(is_odd(position()[0]))
    group = lanes((depth, 128)) // 8
    ends = []
    for high in (False, True):
        items = edge_items(rows, high)
        sides = jnp.zeros((depth, 128), jnp.float32)
        for f, first in ((0, 0), (1, HALO), (2, 2 * HALO)):
            row = items[first][1]
            pack = merged(y1_ref, y2_ref, f, row // 16)
            moved = pltpu.roll(pack, (8 * (first - row)) % 128, 1)
            sides = jnp.where(group >= first, moved, sides)
        ends.append([field_ref[f, row] for f, row in items] + [sides])
    for i, (low, high) in enumerate(zip(*ends)):
        s1_ref[i] = jnp.where(even, high, low)
        s2_ref[i] = jnp.where(even, low, high)


def neighbours_z(b):
    z = lax.broadcasted_iota(jnp.int32, (8, b.shape[1]), 0)
    low, high = b[0:8], b[8:16]
    low_up, high_up = pltpu.roll(low, 1, 0), pltpu.roll(high, 1, 0)
    low_down, high_down = pltpu.roll(low, 7, 0), pltpu.roll(high, 7, 0)
    return jnp.concatenate(
        [
            jnp.where(z == 0, 0.0, low_up) + jnp.where(z == 7, high_down, low_down),
            jnp.where(z == 0, low_up, high_up) + jnp.where(z == 7, 0.0, high_down),
        ],
        axis=0,
    )


def inside_mask(depth):
    pole, poles = position()[1], lax.axis_size("pole")
    lane = lanes((depth, 128))
    return jnp.where(lane < 64, (pole < poles - 1).astype(jnp.float32), (pole > 0).astype(jnp.float32))


def image(before, v, after, diag, inside):
    s = before + after
    p = (3.0 * K) * v + K * s
    e = 3.0 * p + (5.0 * K) * v
    w = e + neighbours_z(p)
    flat = diag * v + (14.0 * K) * s + neighbours_z(e)
    total = flat + pltpu.roll(w, 1, 1) + pltpu.roll(w, 255, 1)
    return jnp.concatenate([total[:, :128], total[:, 128:] * inside], axis=1)


def fold(a):
    return a[0:8, 0:128] + a[8:16, 0:128]


def forms(a, b):
    return fold(a[0] * b[0] - a[1] * b[1]), fold(a[0] * b[1] + a[1] * b[0])


def inner_kernel(field_ref, y1_ref, y2_ref, grown_ref, u1_ref, u2_ref, sums_ref):
    rows, depth = field_ref.shape[1:3]
    for half in range(2):
        packs = [merged(y1_ref, y2_ref, f, half) for f in range(3)]
        for g in range(16):
            row = half * 16 + g
            for f in range(3):
                grown_ref[f, row, :, 0:128] = field_ref[f, row]
                grown_ref[f, row, :, 128:256] = spread(packs[f], g)
    inside = inside_mask(depth)

    def sweep(source, target, reach):
        def step(i, sums):
            x = reach + i
            old = [source[c, x] for c in range(2)]
            new = [image(source[c, x - 1], old[c], source[c, x + 1], grown_ref[2, x], inside) for c in range(2)]
            if target is not None:
                for c in range(2):
                    target[c, x] = new[c]
            return tuple(a + b for a, b in zip(sums, forms(old, old) + forms(old, new)))

        zero = jnp.zeros((8, 128), jnp.float32)
        return lax.fori_loop(0, rows - 2 * reach, step, (zero,) * 4, unroll=True)

    sums = sweep(grown_ref, u1_ref, 1) + sweep(u1_ref, u2_ref, 2) + sweep(u2_ref, None, 3)
    for j, part in enumerate(sums):
        sums_ref[j] = part


def outer_kernel(
    shift_ref, weight_ref, grown_ref, u1_ref, u2_ref, sums_ref, x2_ref, x1_ref, b1_ref, b2_ref, line_ref,
):
    rows, depth = grown_ref.shape[1:3]
    tile, pole = position()
    tiles = lax.axis_size("tile")
    even = jnp.logical_not(is_odd(tile))
    inside = inside_mask(depth)
    sums = [sums_ref[j] for j in range(2 * MOMENTS)]

    def count(j, parts):
        for i, part in enumerate(parts):
            sums[j + i] += part

    def end(high):
        own = (lambda i: rows - 1 + HALO - i) if high else (lambda i: i - HALO)
        there = (tile < tiles - 1) if high else (tile > 0)
        keep = jnp.where(there, inside, 0.0)
        keep = jnp.concatenate([jnp.broadcast_to(there.astype(jnp.float32), inside.shape), keep], axis=1)
        ones = jnp.concatenate([jnp.ones_like(inside), inside], axis=1)
        near, far = (x1_ref, x2_ref) if high else (x2_ref, x1_ref)
        sides = jnp.where(even, near[8], far[8])
        v, diag = [{}, {}], {}
        for item, (f, row) in enumerate(edge_items(rows, not high)):
            value = jnp.concatenate([jnp.where(even, near[item], far[item]), spread(sides, item)], axis=1)
            place = HALO - 1 - row if high else row - (rows - HALO)
            if f < 2:
                v[f][place] = value * there.astype(jnp.float32)
            else:
                diag[place] = value
        for i in range(HALO, 2 * HALO):
            for c in range(2):
                v[c][i] = grown_ref[c, own(i)]
            diag[i] = grown_ref[2, own(i)]

        def powers(source, first, last):
            return [
                {
                    i: image(source[c][i - 1], source[c][i], source[c][i + 1], diag[i], inside)
                    for i in range(first, last)
                }
                for c in range(2)
            ]

        def cut(found):
            for c in range(2):
                for i in found[c]:
                    if i < HALO:
                        found[c][i] = found[c][i] * keep
            return found

        def at(source, i):
            return [source[c][i] for c in range(2)]

        yield
        u1 = cut(powers(v, 1, HALO + 1))
        yield
        for c in range(2):
            for i in range(HALO + 1, HALO + 3):
                u1[c][i] = u1_ref[c, own(i)]
        u2 = cut(powers(u1, 2, HALO + 2))
        yield
        for c in range(2):
            for i in range(HALO + 2, HALO + 4):
                u2[c][i] = u2_ref[c, own(i)]
        u3 = powers(u2, HALO, HALO + 3)
        yield

        count(0, forms(at(v, HALO), at(v, HALO)))
        count(2, forms(at(v, HALO), at(u1, HALO)))
        for i in range(HALO, HALO + 2):
            count(4, forms(at(u1, i), at(u1, i)))
            count(6, forms(at(u1, i), at(u2, i)))
        for i in range(HALO, HALO + 3):
            count(8, forms(at(u2, i), at(u2, i)))
            count(10, forms(at(u2, i), at(u3, i)))
        for c in range(2):
            b1_ref[c, 1 if high else 0] = u1[c][HALO][:, 0:128]
            for i in range(2):
                b2_ref[c, 3 - i if high else i] = u2[c][HALO + i][:, 0:128]
        yield

    for _ in zip(end(False), end(True)):
        pass

    lane = lanes((1, 128))
    line = jnp.zeros((1, 128), jnp.float32)
    for j, part in enumerate(sums):
        line = jnp.where(lane == j, jnp.sum(part, keepdims=True), line)
    mine = shift_ref.shape[0]
    for i in range(mine):
        for c in range(2):
            for base, ref in ((SHIFT_LANE, shift_ref), (WEIGHT_LANE, weight_ref)):
                here = (lane == base + 16 * c + mine * pole + i) & (tile == 0)
                line = jnp.where(here, ref[i:i + 1, c:c + 1], line)
    line_ref[...] = jnp.broadcast_to(line, line_ref.shape)


def mul(a, b):
    return a[0] * b[0] - a[1] * b[1], a[0] * b[1] + a[1] * b[0]


def add(a, b):
    return a[0] + b[0], a[1] + b[1]


def sub(a, b):
    return a[0] - b[0], a[1] - b[1]


def over(a, b):
    norm = b[0] * b[0] + b[1] * b[1]
    factor = jnp.where(norm > 0.0, 1.0 / norm, 0.0)
    return (a[0] * b[0] + a[1] * b[1]) * factor, (a[1] * b[0] - a[0] * b[1]) * factor


def coefficients(line, poles):
    at = lanes((1, 128))

    def spot(j):
        return jnp.sum(jnp.where(at == j, line, 0.0), axis=1, keepdims=True) + jnp.zeros((1, 128), jnp.float32)

    m = [(spot(2 * j), spot(2 * j + 1)) for j in range(MOMENTS)]
    shift = tuple(pltpu.roll(line, (128 - SHIFT_LANE - 16 * c) % 128, 1) for c in range(2))
    weight = tuple(pltpu.roll(line, (128 - WEIGHT_LANE - 16 * c) % 128, 1) for c in range(2))
    scale = 1.0 / jnp.maximum(jnp.abs(m[0][0]), jnp.abs(m[0][1]))
    m = [(re * scale, im * scale) for re, im in m]
    mean = over(m[1], m[0])
    rest = list(m)
    for level in range(1, MOMENTS):
        for j in range(MOMENTS - 1, level - 1, -1):
            rest[j] = sub(rest[j], mul(mean, rest[j - 1]))
    c0, c2, c3, c4, c5 = rest[0], rest[2], rest[3], rest[4], rest[5]
    b1, e1 = over(c2, c0), over(c3, c2)
    d2 = sub(sub(c4, mul(e1, c3)), mul(b1, c2))
    b2 = over(d2, c2)
    e2 = over(sub(sub(sub(c5, mul(e1, c4)), mul(b1, c3)), mul(e1, d2)), d2)
    base = add((shift[1] / TIME_STEP + SIGMA, -shift[0] / TIME_STEP), mean)
    g2 = add(base, e2)
    g1 = sub(mul(add(base, e1), g2), b2)
    source = over((jnp.zeros_like(line), jnp.full_like(line, -1.0 / TIME_STEP)), sub(mul(base, g1), mul(b1, g2)))
    y0, y1, y2 = mul(source, g1), mul((-source[0], -source[1]), g2), source
    k1 = sub(y1, mul(e1, y2))
    k0 = sub(y0, mul(b1, y2))
    k0 = add(sub(k0, mul(mean, k1)), mul(mul(mean, mean), y2))
    twice = mul(mean, y2)
    k1 = sub(k1, (2.0 * twice[0], 2.0 * twice[1]))
    found = []
    for k in (k0, k1, y2):
        term = mul(weight, k)
        found.append(tuple(jnp.sum(jnp.where(at < poles, part, 0.0), axis=1, keepdims=True) for part in term))
    return found


def combine_kernel(poles, field_ref, u1_ref, u2_ref, b1_ref, b2_ref, sums_ref, out_ref, held, sems):
    line = jnp.sum(sums_ref[...], axis=0, keepdims=True)
    k = coefficients(line, poles)
    rows = field_ref.shape[1]
    k = [tuple(jnp.broadcast_to(part, (8, 128)) for part in pair) for pair in k]

    def source(inner, outer, reach, i):
        if i < reach:
            return outer, i
        if i >= rows - reach:
            return outer, i - rows + 2 * reach
        return inner, i

    parts = 2
    copies = []
    for i in range(rows):
        places = ((field_ref, i), source(u1_ref, b1_ref, 1, i), source(u2_ref, b2_ref, 2, i))
        for h in range(field_ref.shape[2] // 8):
            at = slice(8 * h, 8 * h + 8)
            total = None
            for pair, (ref, x) in zip(k, places):
                term = mul(pair, (ref[0, x, at, 0:128], ref[1, x, at, 0:128]))
                total = term if total is None else add(total, term)
            held[0, i, at] = total[0]
            held[1, i, at] = total[1]
        if (i + 1) % (rows // parts) == 0:
            part = pl.ds(i + 1 - rows // parts, rows // parts)
            for c in range(2):
                copy = pltpu.make_async_copy(held.at[c, part], out_ref.at[c, part], sems.at[c, len(copies) // 2])
                copy.start()
                copies.append(copy)
    for copy in copies:
        copy.wait()


def call(kernel, out_shape, specs, scratch=(), flops=0, bytes_accessed=0, aliases={}, out_spec=VMEM):
    return pl.pallas_call(
        kernel,
        out_shape=out_shape,
        in_specs=specs,
        out_specs=jax.tree.map(lambda _: out_spec, out_shape),
        scratch_shapes=list(scratch),
        input_output_aliases=aliases,
        compiler_params=pltpu.CompilerParams(vmem_limit_bytes=32 * 2**20),
        cost_estimate=pl.CostEstimate(flops=flops, bytes_accessed=bytes_accessed, transcendentals=0),
    )


def swaps(axis):
    size = lax.axis_size(axis)
    return [(i, i ^ 1) for i in range(size)], [(i, (i + 1 - 2 * (i % 2 == 0)) % size) for i in range(size)]


def on_device(psi, trap, pole_shift, pole_weight):
    tiles, poles = lax.axis_size("tile"), lax.axis_size("pole")
    rows, depth, width = trap.shape
    f32 = functools.partial(jax.ShapeDtypeStruct, dtype=jnp.float32)

    psi, trap = (pltpu.with_memory_space_constraint(x, pltpu.HBM) for x in (psi, trap))
    message = f32((3, depth, 128))
    m1, m2, field = call(
        load_kernel, (message, message, f32((3, rows, depth, width))), [ANYWHERE] * 2,
        [pltpu.SemaphoreType.DMA((2, 2))],
    )(psi, trap)
    near, across = swaps("pole")
    y2 = lax.ppermute(m2, "pole", across)
    y1 = lax.ppermute(m1, "pole", near)

    edge = f32((3 * HALO, depth, 128))
    s1, s2 = call(edge_kernel, (edge, edge), [VMEM] * 3)(field, y1, y2)
    near, across = swaps("tile")
    x2 = lax.ppermute(s2, "tile", across)
    x1 = lax.ppermute(s1, "tile", near)

    wide = f32((2, rows, depth, 2 * width))
    grown, u1, u2, sums = call(
        inner_kernel,
        (f32((3, rows, depth, 2 * width)), wide, wide, f32((2 * MOMENTS, 8, 128))),
        [VMEM] * 3, flops=20_000_000, bytes_accessed=8_000_000,
    )(field, y1, y2)
    devices = tiles * poles
    b1, b2, line = call(
        outer_kernel,
        (f32((2, 2, depth, width)), f32((2, 4, depth, width)), f32((devices, 128))),
        [VMEM] * 8,
    )(pole_shift, pole_weight, grown, u1, u2, sums, x2, x1)

    lines = lax.all_to_all(line.reshape(devices, 1, 128), ("pole", "tile"), 0, 0, tiled=True)
    combine = functools.partial(combine_kernel, pole_shift.shape[0] * poles)
    return call(
        combine, f32((2, rows, depth, width)), [VMEM] * 6,
        [pltpu.VMEM((2, rows, depth, width), jnp.float32), pltpu.SemaphoreType.DMA((2, 2))], out_spec=ANYWHERE,
    )(field, u1, u2, b1, b2, lines.reshape(devices, 128))


def solution(mesh):
    placed = (
        P(None, "tile", None, "pole"),
        P("tile", None, "pole"),
        P("pole", None),
        P("pole", None),
    )
    return jax.shard_map(
        on_device,
        mesh=mesh,
        in_specs=placed,
        out_specs=P(None, "tile", None, "pole"),
        check_vma=False,
    )
```

```python
import functools

import jax
import jax.numpy as jnp
from jax import lax
from jax.experimental import pallas as pl
from jax.experimental.pallas import tpu as pltpu
from jax.sharding import PartitionSpec as P

COUPLING = 0.5
TIME_STEP = 0.25
SIGMA = 3.0
HALO = 3
K = -0.5 / 30.0
DIAGONAL = -128.0 * K - SIGMA
MOMENTS = 6
SHIFT_LANE, WEIGHT_LANE = 16, 48
VMEM = pl.BlockSpec(memory_space=pltpu.VMEM)
ANYWHERE = pl.BlockSpec(memory_space=pl.ANY)


def lanes(shape):
    return lax.broadcasted_iota(jnp.int32, shape, len(shape) - 1)


def position():
    return lax.axis_index("tile"), lax.axis_index("pole")


def is_odd(index):
    return lax.rem(index, 2) == 1


def load_kernel(psi_ref, trap_ref, s1_ref, s2_ref, field_ref, sems):
    rows, depth = trap_ref.shape[:2]
    half_rows, part_rows = rows // 2, rows // 2
    copies = []
    for part in range(2):
        at = pl.ds(part * part_rows, part_rows)
        pair = (
            pltpu.make_async_copy(psi_ref.at[:, at], field_ref.at[0:2, at], sems.at[part, 0]),
            pltpu.make_async_copy(trap_ref.at[at], field_ref.at[2, at], sems.at[part, 1]),
        )
        for copy in pair:
            copy.start()
        copies.append(pair)
    group = lanes((depth, 128)) // 8
    packs = [[jnp.zeros((depth, 128), jnp.float32)] * 2 for _ in range(3)]
    for row in range(rows):
        half, g = divmod(row, half_rows)
        if g == 0:
            for copy in copies[half]:
                copy.wait()
        re, im = field_ref[0, row], field_ref[1, row]
        diag = field_ref[2, row] + COUPLING * (re * re + im * im) + DIAGONAL
        field_ref[2, row] = diag
        for f, field in enumerate((re, im, diag)):
            moved = pltpu.roll(field, (8 * g + HALO) % 128, 1)
            packs[f][half] = jnp.where(group == g, moved, packs[f][half])
    first = lanes((depth, 128)) % 8 < HALO
    odd = is_odd(position()[1])
    for f in range(3):
        low, high = packs[f]
        to_right = jnp.where(first, low, pltpu.roll(high, HALO, 1))
        to_left = jnp.where(first, pltpu.roll(low, 128 - HALO, 1), high)
        s1_ref[f] = jnp.where(odd, to_left, to_right)
        s2_ref[f] = jnp.where(odd, to_right, to_left)


def merged(y1_ref, y2_ref, f, half):
    odd = is_odd(position()[1])
    first = lanes(y1_ref.shape[1:]) % 8 < HALO
    pole, poles = position()[1], lax.axis_size("pole")
    left = jnp.where(odd, y1_ref[f], y2_ref[f]) * (pole > 0).astype(jnp.float32)
    right = jnp.where(odd, y2_ref[f], y1_ref[f]) * (pole < poles - 1).astype(jnp.float32)
    if half:
        return jnp.where(first, pltpu.roll(left, 128 - HALO, 1), right)
    return jnp.where(first, left, pltpu.roll(right, HALO, 1))


def spread(pack, g):
    return pltpu.roll(pack, (128 - HALO - 8 * g) % 128, 1)


def cell(re, im, trap):
    return trap + COUPLING * (re * re + im * im) + DIAGONAL


def edge_items(high):
    skip = 1 if high else 0
    return [(f, i) for f in range(2) for i in range(HALO)] + [(2, skip + i) for i in range(HALO - 1)]


def end_kernel(psi_ref, trap_ref, s2_ref, s1_ref, raw, sems):
    rows = trap_ref.shape[0]
    copies = []
    for end in range(2):
        at = pl.ds((rows - HALO) * end, HALO)
        copies.append(pltpu.make_async_copy(psi_ref.at[:, at], raw.at[end, 0:2], sems.at[end, 0]))
        copies.append(pltpu.make_async_copy(trap_ref.at[at], raw.at[end, 2], sems.at[end, 1]))
    for copy in copies:
        copy.start()
    for copy in copies:
        copy.wait()
    even = jnp.logical_not(is_odd(position()[0]))
    for item, pair in enumerate(zip(edge_items(False), edge_items(True))):
        low, high = (
            raw[end, f, i] if f < 2 else cell(raw[end, 0, i], raw[end, 1, i], raw[end, 2, i])
            for end, (f, i) in enumerate(pair)
        )
        s1_ref[item] = jnp.where(even, high, low)
        s2_ref[item] = jnp.where(even, low, high)


def corner_kernel(x2_ref, x1_ref, corner_ref):
    items, depth = x1_ref.shape[:2]
    even = jnp.logical_not(is_odd(position()[0]))
    group = lanes((depth, 128)) // 8
    pack = jnp.zeros((depth, 128), jnp.float32)
    for high in (False, True):
        near, far = (x1_ref, x2_ref) if high else (x2_ref, x1_ref)
        for item in range(items):
            g = items + item if high else item
            moved = pltpu.roll(jnp.where(even, near[item], far[item]), (8 * g + HALO) % 128, 1)
            pack = jnp.where(group == g, moved, pack)
    corner_ref[...] = pack


def merged_corners(c1_ref, c2_ref):
    pole, poles = position()[1], lax.axis_size("pole")
    odd = is_odd(pole).astype(jnp.int32)
    first = lanes(c1_ref.shape) % 8 < HALO
    inside = jnp.where(first, (pole > 0).astype(jnp.float32), (pole < poles - 1).astype(jnp.float32))
    return jnp.where(first.astype(jnp.int32) == odd, c1_ref[...], c2_ref[...]) * inside


def neighbours_z(b):
    z = lax.broadcasted_iota(jnp.int32, (8, b.shape[1]), 0)
    low, high = b[0:8], b[8:16]
    low_up, high_up = pltpu.roll(low, 1, 0), pltpu.roll(high, 1, 0)
    low_down, high_down = pltpu.roll(low, 7, 0), pltpu.roll(high, 7, 0)
    return jnp.concatenate(
        [
            jnp.where(z == 0, 0.0, low_up) + jnp.where(z == 7, high_down, low_down),
            jnp.where(z == 0, low_up, high_up) + jnp.where(z == 7, 0.0, high_down),
        ],
        axis=0,
    )


def inside_mask(depth):
    pole, poles = position()[1], lax.axis_size("pole")
    lane = lanes((depth, 128))
    return jnp.where(lane < 64, (pole < poles - 1).astype(jnp.float32), (pole > 0).astype(jnp.float32))


def image(before, v, after, diag, inside):
    s = before + after
    p = (3.0 * K) * v + K * s
    e = 3.0 * p + (5.0 * K) * v
    w = e + neighbours_z(p)
    flat = diag * v + (14.0 * K) * s + neighbours_z(e)
    total = flat + pltpu.roll(w, 1, 1) + pltpu.roll(w, 255, 1)
    return jnp.concatenate([total[:, :128], total[:, 128:] * inside], axis=1)


def fold(a):
    return a[0:8, 0:128] + a[8:16, 0:128]


def forms(a, b):
    return fold(a[0] * b[0] - a[1] * b[1]), fold(a[0] * b[1] + a[1] * b[0])


def sweep(source, target, diag_ref, inside, reach):
    rows = source.shape[1]

    def step(i, sums):
        x = reach + i
        old = [source[c, x] for c in range(2)]
        new = [image(source[c, x - 1], old[c], source[c, x + 1], diag_ref[2, x], inside) for c in range(2)]
        if target is not None:
            for c in range(2):
                target[c, x] = new[c]
        return tuple(a + b for a, b in zip(sums, forms(old, old) + forms(old, new)))

    zero = jnp.zeros((8, 128), jnp.float32)
    return lax.fori_loop(0, rows - 2 * reach, step, (zero,) * 4, unroll=True)


def first_kernel(field_ref, y1_ref, y2_ref, grown_ref, u1_ref, sums_ref):
    rows, depth = field_ref.shape[1:3]
    for half in range(2):
        packs = [merged(y1_ref, y2_ref, f, half) for f in range(3)]
        for g in range(16):
            row = half * 16 + g
            for f in range(3):
                grown_ref[f, row, :, 0:128] = field_ref[f, row]
                grown_ref[f, row, :, 128:256] = spread(packs[f], g)
    inside = inside_mask(depth)
    sums = sweep(grown_ref, u1_ref, grown_ref, inside, 1)
    for j, part in enumerate(sums):
        sums_ref[j] = part


def second_kernel(grown_ref, u1_ref, u2_ref, sums_ref):
    inside = inside_mask(grown_ref.shape[2])
    sums = sweep(u1_ref, u2_ref, grown_ref, inside, 2) + sweep(u2_ref, None, grown_ref, inside, 3)
    for j, part in enumerate(sums):
        sums_ref[j] = part


def outer_kernel(
    shift_ref, weight_ref, grown_ref, u1_ref, u2_ref, sums1_ref, sums2_ref, x2_ref, x1_ref, c2_ref, c1_ref,
    b1_ref, b2_ref, line_ref,
):
    rows, depth = grown_ref.shape[1:3]
    tile, pole = position()
    tiles = lax.axis_size("tile")
    even = jnp.logical_not(is_odd(tile))
    inside = inside_mask(depth)
    sums = [ref[j] for ref in (sums1_ref, sums2_ref) for j in range(ref.shape[0])]
    corners = merged_corners(c1_ref, c2_ref)

    def count(j, parts):
        for i, part in enumerate(parts):
            sums[j + i] += part

    def end(high):
        own = (lambda i: rows - 1 + HALO - i) if high else (lambda i: i - HALO)
        there = (tile < tiles - 1) if high else (tile > 0)
        keep = jnp.where(there, inside, 0.0)
        keep = jnp.concatenate([jnp.broadcast_to(there.astype(jnp.float32), inside.shape), keep], axis=1)
        ones = jnp.concatenate([jnp.ones_like(inside), inside], axis=1)
        near, far = (x1_ref, x2_ref) if high else (x2_ref, x1_ref)
        v, diag = [{}, {}], {}
        items = edge_items(not high)
        for item, (f, i) in enumerate(items):
            side = spread(corners, len(items) + item if high else item)
            value = jnp.concatenate([jnp.where(even, near[item], far[item]), side], axis=1)
            place = HALO - 1 - i if high else i
            if f < 2:
                v[f][place] = value * there.astype(jnp.float32)
            else:
                diag[place] = value
        for i in range(HALO, 2 * HALO):
            for c in range(2):
                v[c][i] = grown_ref[c, own(i)]
            diag[i] = grown_ref[2, own(i)]

        def powers(source, first, last):
            return [
                {
                    i: image(source[c][i - 1], source[c][i], source[c][i + 1], diag[i], inside)
                    for i in range(first, last)
                }
                for c in range(2)
            ]

        def cut(found):
            for c in range(2):
                for i in found[c]:
                    if i < HALO:
                        found[c][i] = found[c][i] * keep
            return found

        def at(source, i):
            return [source[c][i] for c in range(2)]

        yield
        u1 = cut(powers(v, 1, HALO + 1))
        yield
        for c in range(2):
            for i in range(HALO + 1, HALO + 3):
                u1[c][i] = u1_ref[c, own(i)]
        u2 = cut(powers(u1, 2, HALO + 2))
        yield
        for c in range(2):
            for i in range(HALO + 2, HALO + 4):
                u2[c][i] = u2_ref[c, own(i)]
        u3 = powers(u2, HALO, HALO + 3)
        yield

        count(0, forms(at(v, HALO), at(v, HALO)))
        count(2, forms(at(v, HALO), at(u1, HALO)))
        for i in range(HALO, HALO + 2):
            count(4, forms(at(u1, i), at(u1, i)))
            count(6, forms(at(u1, i), at(u2, i)))
        for i in range(HALO, HALO + 3):
            count(8, forms(at(u2, i), at(u2, i)))
            count(10, forms(at(u2, i), at(u3, i)))
        for c in range(2):
            b1_ref[c, 1 if high else 0] = u1[c][HALO][:, 0:128]
            for i in range(2):
                b2_ref[c, 3 - i if high else i] = u2[c][HALO + i][:, 0:128]
        yield

    for _ in zip(end(False), end(True)):
        pass

    lane = lanes((1, 128))
    line = jnp.zeros((1, 128), jnp.float32)
    for j, part in enumerate(sums):
        line = jnp.where(lane == j, jnp.sum(part, keepdims=True), line)
    mine = shift_ref.shape[0]
    for i in range(mine):
        for c in range(2):
            for base, ref in ((SHIFT_LANE, shift_ref), (WEIGHT_LANE, weight_ref)):
                here = (lane == base + 16 * c + mine * pole + i) & (tile == 0)
                line = jnp.where(here, ref[i:i + 1, c:c + 1], line)
    line_ref[...] = jnp.broadcast_to(line, line_ref.shape)


def mul(a, b):
    return a[0] * b[0] - a[1] * b[1], a[0] * b[1] + a[1] * b[0]


def add(a, b):
    return a[0] + b[0], a[1] + b[1]


def sub(a, b):
    return a[0] - b[0], a[1] - b[1]


def over(a, b):
    norm = b[0] * b[0] + b[1] * b[1]
    factor = jnp.where(norm > 0.0, 1.0 / norm, 0.0)
    return (a[0] * b[0] + a[1] * b[1]) * factor, (a[1] * b[0] - a[0] * b[1]) * factor


def coefficients(line, poles):
    at = lanes((1, 128))

    def spot(j):
        return jnp.sum(jnp.where(at == j, line, 0.0), axis=1, keepdims=True) + jnp.zeros((1, 128), jnp.float32)

    m = [(spot(2 * j), spot(2 * j + 1)) for j in range(MOMENTS)]
    shift = tuple(pltpu.roll(line, (128 - SHIFT_LANE - 16 * c) % 128, 1) for c in range(2))
    weight = tuple(pltpu.roll(line, (128 - WEIGHT_LANE - 16 * c) % 128, 1) for c in range(2))
    scale = 1.0 / jnp.maximum(jnp.abs(m[0][0]), jnp.abs(m[0][1]))
    m = [(re * scale, im * scale) for re, im in m]
    mean = over(m[1], m[0])
    rest = list(m)
    for level in range(1, MOMENTS):
        for j in range(MOMENTS - 1, level - 1, -1):
            rest[j] = sub(rest[j], mul(mean, rest[j - 1]))
    c0, c2, c3, c4, c5 = rest[0], rest[2], rest[3], rest[4], rest[5]
    b1, e1 = over(c2, c0), over(c3, c2)
    d2 = sub(sub(c4, mul(e1, c3)), mul(b1, c2))
    b2 = over(d2, c2)
    e2 = over(sub(sub(sub(c5, mul(e1, c4)), mul(b1, c3)), mul(e1, d2)), d2)
    base = add((shift[1] / TIME_STEP + SIGMA, -shift[0] / TIME_STEP), mean)
    g2 = add(base, e2)
    g1 = sub(mul(add(base, e1), g2), b2)
    source = over((jnp.zeros_like(line), jnp.full_like(line, -1.0 / TIME_STEP)), sub(mul(base, g1), mul(b1, g2)))
    y0, y1, y2 = mul(source, g1), mul((-source[0], -source[1]), g2), source
    k1 = sub(y1, mul(e1, y2))
    k0 = sub(y0, mul(b1, y2))
    k0 = add(sub(k0, mul(mean, k1)), mul(mul(mean, mean), y2))
    twice = mul(mean, y2)
    k1 = sub(k1, (2.0 * twice[0], 2.0 * twice[1]))
    found = []
    for k in (k0, k1, y2):
        term = mul(weight, k)
        found.append(tuple(jnp.sum(jnp.where(at < poles, part, 0.0), axis=1, keepdims=True) for part in term))
    return found


def combine_kernel(poles, field_ref, u1_ref, u2_ref, b1_ref, b2_ref, sums_ref, out_ref, held, sems):
    line = jnp.sum(sums_ref[...], axis=0, keepdims=True)
    k = coefficients(line, poles)
    rows = field_ref.shape[1]
    k = [tuple(jnp.broadcast_to(part, (8, 128)) for part in pair) for pair in k]

    def source(inner, outer, reach, i):
        if i < reach:
            return outer, i
        if i >= rows - reach:
            return outer, i - rows + 2 * reach
        return inner, i

    parts = 2
    copies = []
    for i in range(rows):
        places = ((field_ref, i), source(u1_ref, b1_ref, 1, i), source(u2_ref, b2_ref, 2, i))
        for h in range(field_ref.shape[2] // 8):
            at = slice(8 * h, 8 * h + 8)
            total = None
            for pair, (ref, x) in zip(k, places):
                term = mul(pair, (ref[0, x, at, 0:128], ref[1, x, at, 0:128]))
                total = term if total is None else add(total, term)
            held[0, i, at] = total[0]
            held[1, i, at] = total[1]
        if (i + 1) % (rows // parts) == 0:
            part = pl.ds(i + 1 - rows // parts, rows // parts)
            for c in range(2):
                copy = pltpu.make_async_copy(held.at[c, part], out_ref.at[c, part], sems.at[c, len(copies) // 2])
                copy.start()
                copies.append(copy)
    for copy in copies:
        copy.wait()


def call(kernel, out_shape, specs, scratch=(), flops=0, bytes_accessed=0, aliases={}, out_spec=VMEM):
    return pl.pallas_call(
        kernel,
        out_shape=out_shape,
        in_specs=specs,
        out_specs=jax.tree.map(lambda _: out_spec, out_shape),
        scratch_shapes=list(scratch),
        input_output_aliases=aliases,
        compiler_params=pltpu.CompilerParams(vmem_limit_bytes=32 * 2**20),
        cost_estimate=pl.CostEstimate(flops=flops, bytes_accessed=bytes_accessed, transcendentals=0),
    )


def swaps(axis):
    size = lax.axis_size(axis)
    return [(i, i ^ 1) for i in range(size)], [(i, (i + 1 - 2 * (i % 2 == 0)) % size) for i in range(size)]


def on_device(psi, trap, pole_shift, pole_weight):
    tiles, poles = lax.axis_size("tile"), lax.axis_size("pole")
    rows, depth, width = trap.shape
    f32 = functools.partial(jax.ShapeDtypeStruct, dtype=jnp.float32)

    psi, trap = (pltpu.with_memory_space_constraint(x, pltpu.HBM) for x in (psi, trap))
    edge = f32((3 * HALO - 1, depth, width))
    s2, s1 = call(
        end_kernel, (edge, edge), [ANYWHERE] * 2,
        [pltpu.VMEM((2, 3, HALO, depth, width), jnp.float32), pltpu.SemaphoreType.DMA((2, 2))],
    )(psi, trap)
    near, across = swaps("tile")
    pairs = []
    for pole in range(poles):
        for tile, other in across:
            pairs.append((pole * tiles + tile, (pole * tiles + other) if abs(tile - other) == 1 else ((pole ^ 1) * tiles + tile)))
    x2 = lax.ppermute(s2, ("pole", "tile"), pairs)
    x1 = lax.ppermute(s1, "tile", near)

    message = f32((3, depth, 128))
    m1, m2, field = call(
        load_kernel, (message, message, f32((3, rows, depth, width))), [ANYWHERE] * 2,
        [pltpu.SemaphoreType.DMA((2, 2))],
    )(psi, trap)
    pole_near, pole_across = swaps("pole")
    y2 = lax.ppermute(m2, "pole", pole_across)
    y1 = lax.ppermute(m1, "pole", pole_near)

    wide = f32((2, rows, depth, 2 * width))
    grown, u1, sums1 = call(
        first_kernel,
        (f32((3, rows, depth, 2 * width)), wide, f32((4, 8, 128))),
        [VMEM] * 3, flops=8_000_000, bytes_accessed=3_000_000,
    )(field, y1, y2)
    x2, x1, sums1 = lax.optimization_barrier((x2, x1, sums1))
    corner = call(corner_kernel, f32((depth, 128)), [VMEM] * 2)(x2, x1)
    c2 = lax.ppermute(corner, "pole", pole_across)
    c1 = lax.ppermute(corner, "pole", pole_near)

    u2, sums2 = call(
        second_kernel, (wide, f32((8, 8, 128))), [VMEM] * 2, flops=12_000_000, bytes_accessed=5_000_000,
    )(grown, u1)

    devices = tiles * poles
    b1, b2, line = call(
        outer_kernel,
        (f32((2, 2, depth, width)), f32((2, 4, depth, width)), f32((devices, 128))),
        [VMEM] * 11,
    )(pole_shift, pole_weight, grown, u1, u2, sums1, sums2, x2, x1, c2, c1)

    lines = lax.all_to_all(line.reshape(devices, 1, 128), ("pole", "tile"), 0, 0, tiled=True)
    combine = functools.partial(combine_kernel, pole_shift.shape[0] * poles)
    return call(
        combine, f32((2, rows, depth, width)), [VMEM] * 6,
        [pltpu.VMEM((2, rows, depth, width), jnp.float32), pltpu.SemaphoreType.DMA((2, 2))], out_spec=ANYWHERE,
    )(field, u1, u2, b1, b2, lines.reshape(devices, 128))


def solution(mesh):
    placed = (
        P(None, "tile", None, "pole"),
        P("tile", None, "pole"),
        P("pole", None),
        P("pole", None),
    )
    return jax.shard_map(
        on_device,
        mesh=mesh,
        in_specs=placed,
        out_specs=P(None, "tile", None, "pole"),
        check_vma=False,
    )
```

```python
import functools

import jax
import jax.numpy as jnp
from jax import lax
from jax.experimental import pallas as pl
from jax.experimental.pallas import tpu as pltpu
from jax.sharding import PartitionSpec as P

COUPLING = 0.5
TIME_STEP = 0.25
SIGMA = 3.0
HALO = 3
K = -0.5 / 30.0
DIAGONAL = -128.0 * K - SIGMA
MOMENTS = 6
SHIFT_LANE, WEIGHT_LANE = 16, 48
VMEM = pl.BlockSpec(memory_space=pltpu.VMEM)
ANYWHERE = pl.BlockSpec(memory_space=pl.ANY)


def lanes(shape):
    return lax.broadcasted_iota(jnp.int32, shape, len(shape) - 1)


def position():
    return lax.axis_index("tile"), lax.axis_index("pole")


def is_odd(index):
    return lax.rem(index, 2) == 1


def load_kernel(psi_ref, trap_ref, s1_ref, s2_ref, field_ref):
    rows, depth = trap_ref.shape[:2]
    half_rows = rows // 2
    group = lanes((depth, 128)) // 8
    packs = [[jnp.zeros((depth, 128), jnp.float32)] * 2 for _ in range(3)]
    for row in range(rows):
        half, g = divmod(row, half_rows)
        re, im = psi_ref[0, row], psi_ref[1, row]
        diag = cell(re, im, trap_ref[row])
        for f, field in enumerate((re, im, diag)):
            field_ref[f, row] = field
            moved = pltpu.roll(field, (8 * g + HALO) % 128, 1)
            packs[f][half] = jnp.where(group == g, moved, packs[f][half])
    first = lanes((depth, 128)) % 8 < HALO
    odd = is_odd(position()[1])
    for f in range(3):
        low, high = packs[f]
        to_right = jnp.where(first, low, pltpu.roll(high, HALO, 1))
        to_left = jnp.where(first, pltpu.roll(low, 128 - HALO, 1), high)
        s1_ref[f] = jnp.where(odd, to_left, to_right)
        s2_ref[f] = jnp.where(odd, to_right, to_left)


def merged(y1_ref, y2_ref, f, half):
    odd = is_odd(position()[1])
    first = lanes(y1_ref.shape[1:]) % 8 < HALO
    pole, poles = position()[1], lax.axis_size("pole")
    left = jnp.where(odd, y1_ref[f], y2_ref[f]) * (pole > 0).astype(jnp.float32)
    right = jnp.where(odd, y2_ref[f], y1_ref[f]) * (pole < poles - 1).astype(jnp.float32)
    if half:
        return jnp.where(first, pltpu.roll(left, 128 - HALO, 1), right)
    return jnp.where(first, left, pltpu.roll(right, HALO, 1))


def spread(pack, g):
    return pltpu.roll(pack, (128 - HALO - 8 * g) % 128, 1)


def cell(re, im, trap):
    return trap + COUPLING * (re * re + im * im) + DIAGONAL


def edge_items(high):
    skip = 1 if high else 0
    return [(f, i) for f in range(2) for i in range(HALO)] + [(2, skip + i) for i in range(HALO - 1)]


def end_kernel(psi_ref, trap_ref, s2_ref, s1_ref, raw, sems):
    rows = trap_ref.shape[0]
    copies = []
    for end in range(2):
        at = pl.ds((rows - HALO) * end, HALO)
        copies.append(pltpu.make_async_copy(psi_ref.at[:, at], raw.at[end, 0:2], sems.at[end, 0]))
        copies.append(pltpu.make_async_copy(trap_ref.at[at], raw.at[end, 2], sems.at[end, 1]))
    for copy in copies:
        copy.start()
    for copy in copies:
        copy.wait()
    even = jnp.logical_not(is_odd(position()[0]))
    for item, pair in enumerate(zip(edge_items(False), edge_items(True))):
        low, high = (
            raw[end, f, i] if f < 2 else cell(raw[end, 0, i], raw[end, 1, i], raw[end, 2, i])
            for end, (f, i) in enumerate(pair)
        )
        s1_ref[item] = jnp.where(even, high, low)
        s2_ref[item] = jnp.where(even, low, high)


def corner_kernel(x2_ref, x1_ref, corner_ref):
    items, depth = x1_ref.shape[:2]
    even = jnp.logical_not(is_odd(position()[0]))
    group = lanes((depth, 128)) // 8
    pack = jnp.zeros((depth, 128), jnp.float32)
    for high in (False, True):
        near, far = (x1_ref, x2_ref) if high else (x2_ref, x1_ref)
        for item in range(items):
            g = items + item if high else item
            moved = pltpu.roll(jnp.where(even, near[item], far[item]), (8 * g + HALO) % 128, 1)
            pack = jnp.where(group == g, moved, pack)
    corner_ref[...] = pack


def merged_corners(c1_ref, c2_ref):
    pole, poles = position()[1], lax.axis_size("pole")
    odd = is_odd(pole).astype(jnp.int32)
    first = lanes(c1_ref.shape) % 8 < HALO
    inside = jnp.where(first, (pole > 0).astype(jnp.float32), (pole < poles - 1).astype(jnp.float32))
    return jnp.where(first.astype(jnp.int32) == odd, c1_ref[...], c2_ref[...]) * inside


def neighbours_z(b):
    z = lax.broadcasted_iota(jnp.int32, (8, b.shape[1]), 0)
    low, high = b[0:8], b[8:16]
    low_up, high_up = pltpu.roll(low, 1, 0), pltpu.roll(high, 1, 0)
    low_down, high_down = pltpu.roll(low, 7, 0), pltpu.roll(high, 7, 0)
    return jnp.concatenate(
        [
            jnp.where(z == 0, 0.0, low_up) + jnp.where(z == 7, high_down, low_down),
            jnp.where(z == 0, low_up, high_up) + jnp.where(z == 7, 0.0, high_down),
        ],
        axis=0,
    )


def inside_mask(depth):
    pole, poles = position()[1], lax.axis_size("pole")
    lane = lanes((depth, 128))
    return jnp.where(lane < 64, (pole < poles - 1).astype(jnp.float32), (pole > 0).astype(jnp.float32))


def image(before, v, after, diag, inside):
    s = before + after
    p = (3.0 * K) * v + K * s
    e = 3.0 * p + (5.0 * K) * v
    w = e + neighbours_z(p)
    flat = diag * v + (14.0 * K) * s + neighbours_z(e)
    total = flat + pltpu.roll(w, 1, 1) + pltpu.roll(w, 255, 1)
    return jnp.concatenate([total[:, :128], total[:, 128:] * inside], axis=1)


def fold(a):
    return a[0:8, 0:128] + a[8:16, 0:128]


def forms(a, b):
    return fold(a[0] * b[0] - a[1] * b[1]), fold(a[0] * b[1] + a[1] * b[0])


def sweep(source, target, diag_ref, inside, reach):
    rows = source.shape[1]

    def step(i, sums):
        x = reach + i
        old = [source[c, x] for c in range(2)]
        new = [image(source[c, x - 1], old[c], source[c, x + 1], diag_ref[2, x], inside) for c in range(2)]
        if target is not None:
            for c in range(2):
                target[c, x] = new[c]
        return tuple(a + b for a, b in zip(sums, forms(old, old) + forms(old, new)))

    zero = jnp.zeros((8, 128), jnp.float32)
    return lax.fori_loop(0, rows - 2 * reach, step, (zero,) * 4, unroll=True)


def first_kernel(field_ref, y2_ref, y1_ref, grown_ref, u1_ref, sums_ref):
    rows, depth = field_ref.shape[1:3]
    for half in range(2):
        packs = [merged(y1_ref, y2_ref, f, half) for f in range(3)]
        for g in range(16):
            row = half * 16 + g
            for f in range(3):
                grown_ref[f, row, :, 0:128] = field_ref[f, row]
                grown_ref[f, row, :, 128:256] = spread(packs[f], g)
    inside = inside_mask(depth)
    sums = sweep(grown_ref, u1_ref, grown_ref, inside, 1)
    for j, part in enumerate(sums):
        sums_ref[j] = part


def second_kernel(grown_ref, u1_ref, u2_ref, sums_ref):
    inside = inside_mask(grown_ref.shape[2])
    sums = sweep(u1_ref, u2_ref, grown_ref, inside, 2) + sweep(u2_ref, None, grown_ref, inside, 3)
    for j, part in enumerate(sums):
        sums_ref[j] = part


def outer_kernel(
    shift_ref, weight_ref, grown_ref, u1_ref, u2_ref, sums1_ref, sums2_ref, x2_ref, x1_ref, c1_ref, c2_ref,
    b1_ref, b2_ref, line_ref,
):
    rows, depth = grown_ref.shape[1:3]
    tile, pole = position()
    tiles = lax.axis_size("tile")
    even = jnp.logical_not(is_odd(tile))
    inside = inside_mask(depth)
    sums = [ref[j] for ref in (sums1_ref, sums2_ref) for j in range(ref.shape[0])]
    corners = merged_corners(c1_ref, c2_ref)

    def count(j, parts):
        for i, part in enumerate(parts):
            sums[j + i] += part

    def end(high):
        own = (lambda i: rows - 1 + HALO - i) if high else (lambda i: i - HALO)
        there = (tile < tiles - 1) if high else (tile > 0)
        keep = jnp.where(there, inside, 0.0)
        keep = jnp.concatenate([jnp.broadcast_to(there.astype(jnp.float32), inside.shape), keep], axis=1)
        ones = jnp.concatenate([jnp.ones_like(inside), inside], axis=1)
        near, far = (x1_ref, x2_ref) if high else (x2_ref, x1_ref)
        v, diag = [{}, {}], {}
        items = edge_items(not high)
        for item, (f, i) in enumerate(items):
            side = spread(corners, len(items) + item if high else item)
            value = jnp.concatenate([jnp.where(even, near[item], far[item]), side], axis=1)
            place = HALO - 1 - i if high else i
            if f < 2:
                v[f][place] = value * there.astype(jnp.float32)
            else:
                diag[place] = value
        for i in range(HALO, 2 * HALO):
            for c in range(2):
                v[c][i] = grown_ref[c, own(i)]
            diag[i] = grown_ref[2, own(i)]

        def powers(source, first, last):
            return [
                {
                    i: image(source[c][i - 1], source[c][i], source[c][i + 1], diag[i], inside)
                    for i in range(first, last)
                }
                for c in range(2)
            ]

        def cut(found):
            for c in range(2):
                for i in found[c]:
                    if i < HALO:
                        found[c][i] = found[c][i] * keep
            return found

        def at(source, i):
            return [source[c][i] for c in range(2)]

        yield
        u1 = cut(powers(v, 1, HALO + 1))
        yield
        for c in range(2):
            for i in range(HALO + 1, HALO + 3):
                u1[c][i] = u1_ref[c, own(i)]
        u2 = cut(powers(u1, 2, HALO + 2))
        yield
        for c in range(2):
            for i in range(HALO + 2, HALO + 4):
                u2[c][i] = u2_ref[c, own(i)]
        u3 = powers(u2, HALO, HALO + 3)
        yield

        count(0, forms(at(v, HALO), at(v, HALO)))
        count(2, forms(at(v, HALO), at(u1, HALO)))
        for i in range(HALO, HALO + 2):
            count(4, forms(at(u1, i), at(u1, i)))
            count(6, forms(at(u1, i), at(u2, i)))
        for i in range(HALO, HALO + 3):
            count(8, forms(at(u2, i), at(u2, i)))
            count(10, forms(at(u2, i), at(u3, i)))
        for c in range(2):
            b1_ref[c, 1 if high else 0] = u1[c][HALO][:, 0:128]
            for i in range(2):
                b2_ref[c, 3 - i if high else i] = u2[c][HALO + i][:, 0:128]
        yield

    for _ in zip(end(False), end(True)):
        pass

    lane = lanes((1, 128))
    line = jnp.zeros((1, 128), jnp.float32)
    for j, part in enumerate(sums):
        line = jnp.where(lane == j, jnp.sum(part, keepdims=True), line)
    mine = shift_ref.shape[0]
    for i in range(mine):
        for c in range(2):
            for base, ref in ((SHIFT_LANE, shift_ref), (WEIGHT_LANE, weight_ref)):
                here = (lane == base + 16 * c + mine * pole + i) & (tile == 0)
                line = jnp.where(here, ref[i:i + 1, c:c + 1], line)
    line_ref[...] = jnp.broadcast_to(line, line_ref.shape)


def mul(a, b):
    return a[0] * b[0] - a[1] * b[1], a[0] * b[1] + a[1] * b[0]


def add(a, b):
    return a[0] + b[0], a[1] + b[1]


def sub(a, b):
    return a[0] - b[0], a[1] - b[1]


def over(a, b):
    norm = b[0] * b[0] + b[1] * b[1]
    factor = jnp.where(norm > 0.0, 1.0 / norm, 0.0)
    return (a[0] * b[0] + a[1] * b[1]) * factor, (a[1] * b[0] - a[0] * b[1]) * factor


def coefficients(line, poles):
    at = lanes((1, 128))

    def spot(j):
        return jnp.sum(jnp.where(at == j, line, 0.0), axis=1, keepdims=True) + jnp.zeros((1, 128), jnp.float32)

    m = [(spot(2 * j), spot(2 * j + 1)) for j in range(MOMENTS)]
    shift = tuple(pltpu.roll(line, (128 - SHIFT_LANE - 16 * c) % 128, 1) for c in range(2))
    weight = tuple(pltpu.roll(line, (128 - WEIGHT_LANE - 16 * c) % 128, 1) for c in range(2))
    scale = 1.0 / jnp.maximum(jnp.abs(m[0][0]), jnp.abs(m[0][1]))
    m = [(re * scale, im * scale) for re, im in m]
    mean = over(m[1], m[0])
    rest = list(m)
    for level in range(1, MOMENTS):
        for j in range(MOMENTS - 1, level - 1, -1):
            rest[j] = sub(rest[j], mul(mean, rest[j - 1]))
    c0, c2, c3, c4, c5 = rest[0], rest[2], rest[3], rest[4], rest[5]
    b1, e1 = over(c2, c0), over(c3, c2)
    d2 = sub(sub(c4, mul(e1, c3)), mul(b1, c2))
    b2 = over(d2, c2)
    e2 = over(sub(sub(sub(c5, mul(e1, c4)), mul(b1, c3)), mul(e1, d2)), d2)
    base = add((shift[1] / TIME_STEP + SIGMA, -shift[0] / TIME_STEP), mean)
    g2 = add(base, e2)
    g1 = sub(mul(add(base, e1), g2), b2)
    source = over((jnp.zeros_like(line), jnp.full_like(line, -1.0 / TIME_STEP)), sub(mul(base, g1), mul(b1, g2)))
    y0, y1, y2 = mul(source, g1), mul((-source[0], -source[1]), g2), source
    k1 = sub(y1, mul(e1, y2))
    k0 = sub(y0, mul(b1, y2))
    k0 = add(sub(k0, mul(mean, k1)), mul(mul(mean, mean), y2))
    twice = mul(mean, y2)
    k1 = sub(k1, (2.0 * twice[0], 2.0 * twice[1]))
    found = []
    for k in (k0, k1, y2):
        term = mul(weight, k)
        found.append(tuple(jnp.sum(jnp.where(at < poles, part, 0.0), axis=1, keepdims=True) for part in term))
    return found


def combine_kernel(poles, field_ref, u1_ref, u2_ref, b1_ref, b2_ref, sums_ref, out_ref, held, sems):
    line = jnp.sum(sums_ref[...], axis=0, keepdims=True)
    k = coefficients(line, poles)
    rows = field_ref.shape[1]
    k = [tuple(jnp.broadcast_to(part, (8, 128)) for part in pair) for pair in k]

    def source(inner, outer, reach, i):
        if i < reach:
            return outer, i
        if i >= rows - reach:
            return outer, i - rows + 2 * reach
        return inner, i

    parts = 2
    copies = []
    for i in range(rows):
        places = ((field_ref, i), source(u1_ref, b1_ref, 1, i), source(u2_ref, b2_ref, 2, i))
        for h in range(field_ref.shape[2] // 8):
            at = slice(8 * h, 8 * h + 8)
            total = None
            for pair, (ref, x) in zip(k, places):
                term = mul(pair, (ref[0, x, at, 0:128], ref[1, x, at, 0:128]))
                total = term if total is None else add(total, term)
            held[0, i, at] = total[0]
            held[1, i, at] = total[1]
        if (i + 1) % (rows // parts) == 0:
            part = pl.ds(i + 1 - rows // parts, rows // parts)
            for c in range(2):
                copy = pltpu.make_async_copy(held.at[c, part], out_ref.at[c, part], sems.at[c, len(copies) // 2])
                copy.start()
                copies.append(copy)
    for copy in copies:
        copy.wait()


def call(kernel, out_shape, specs, scratch=(), flops=0, bytes_accessed=0, aliases={}, out_spec=VMEM):
    return pl.pallas_call(
        kernel,
        out_shape=out_shape,
        in_specs=specs,
        out_specs=jax.tree.map(lambda _: out_spec, out_shape),
        scratch_shapes=list(scratch),
        input_output_aliases=aliases,
        compiler_params=pltpu.CompilerParams(vmem_limit_bytes=32 * 2**20),
        cost_estimate=pl.CostEstimate(flops=flops, bytes_accessed=bytes_accessed, transcendentals=0),
    )


def swaps(axis):
    size = lax.axis_size(axis)
    return [(i, i ^ 1) for i in range(size)], [(i, (i + 1 - 2 * (i % 2 == 0)) % size) for i in range(size)]


def on_device(psi, trap, pole_shift, pole_weight):
    tiles, poles = lax.axis_size("tile"), lax.axis_size("pole")
    rows, depth, width = trap.shape
    f32 = functools.partial(jax.ShapeDtypeStruct, dtype=jnp.float32)

    edge = f32((3 * HALO - 1, depth, width))
    s2, s1 = call(
        end_kernel, (edge, edge), [ANYWHERE] * 2,
        [pltpu.VMEM((2, 3, HALO, depth, width), jnp.float32), pltpu.SemaphoreType.DMA((2, 2))],
        flops=2_000_000_000, bytes_accessed=40_000_000,
    )(*(pltpu.with_memory_space_constraint(x, pltpu.HBM) for x in (psi, trap)))
    near, across = swaps("tile")
    pairs = []
    for pole in range(poles):
        for tile, other in across:
            pairs.append((pole * tiles + tile, (pole * tiles + other) if abs(tile - other) == 1 else ((pole ^ 1) * tiles + tile)))
    x2 = lax.ppermute(s2, ("pole", "tile"), pairs)
    x1 = lax.ppermute(s1, "tile", near)

    message = f32((3, depth, 128))
    m1, m2, field = call(
        load_kernel, (message, message, f32((3, rows, depth, width))), [VMEM] * 2,
    )(psi, trap)
    pole_near, pole_across = swaps("pole")
    y2 = lax.ppermute(m2, "pole", pole_across)
    y1 = lax.ppermute(m1, "pole", pole_near)

    wide = f32((2, rows, depth, 2 * width))
    grown, u1, sums1 = call(
        first_kernel,
        (f32((3, rows, depth, 2 * width)), wide, f32((4, 8, 128))),
        [VMEM] * 3, flops=8_000_000, bytes_accessed=3_000_000,
    )(field, y2, y1)
    x2, x1, sums1 = lax.optimization_barrier((x2, x1, sums1))
    corner = call(corner_kernel, f32((depth, 128)), [VMEM] * 2)(x2, x1)
    c2 = lax.ppermute(corner, "pole", pole_across)
    c1 = lax.ppermute(corner, "pole", pole_near)

    u2, sums2 = call(
        second_kernel, (wide, f32((8, 8, 128))), [VMEM] * 2, flops=12_000_000, bytes_accessed=5_000_000,
    )(grown, u1)

    devices = tiles * poles
    b1, b2, line = call(
        outer_kernel,
        (f32((2, 2, depth, width)), f32((2, 4, depth, width)), f32((devices, 128))),
        [VMEM] * 11,
    )(pole_shift, pole_weight, grown, u1, u2, sums1, sums2, x2, x1, c1, c2)

    lines = lax.all_to_all(line.reshape(devices, 1, 128), ("pole", "tile"), 0, 0, tiled=True)
    combine = functools.partial(combine_kernel, pole_shift.shape[0] * poles)
    return call(
        combine, f32((2, rows, depth, width)), [VMEM] * 6,
        [pltpu.VMEM((2, rows, depth, width), jnp.float32), pltpu.SemaphoreType.DMA((2, 2))], out_spec=ANYWHERE,
    )(field, u1, u2, b1, b2, lines.reshape(devices, 128))


def solution(mesh):
    placed = (
        P(None, "tile", None, "pole"),
        P("tile", None, "pole"),
        P("pole", None),
        P("pole", None),
    )
    return jax.shard_map(
        on_device,
        mesh=mesh,
        in_specs=placed,
        out_specs=P(None, "tile", None, "pole"),
        check_vma=False,
    )
```

```python
import functools

import jax
import jax.numpy as jnp
from jax import lax
from jax.experimental import pallas as pl
from jax.experimental.pallas import tpu as pltpu
from jax.sharding import PartitionSpec as P

COUPLING = 0.5
TIME_STEP = 0.25
SIGMA = 3.0
HALO = 3
K = -0.5 / 30.0
DIAGONAL = -128.0 * K - SIGMA
MOMENTS = 6
SHIFT_LANE, WEIGHT_LANE = 16, 48
VMEM = pl.BlockSpec(memory_space=pltpu.VMEM)
ANYWHERE = pl.BlockSpec(memory_space=pl.ANY)


def lanes(shape):
    return lax.broadcasted_iota(jnp.int32, shape, len(shape) - 1)


def position():
    return lax.axis_index("tile"), lax.axis_index("pole")


def is_odd(index):
    return lax.rem(index, 2) == 1


def load_kernel(psi_ref, trap_ref, s1_ref, s2_ref, field_ref):
    rows, depth = trap_ref.shape[:2]
    half_rows = rows // 2
    group = lanes((depth, 128)) // 8
    packs = [[jnp.zeros((depth, 128), jnp.float32)] * 2 for _ in range(3)]
    for row in range(rows):
        half, g = divmod(row, half_rows)
        re, im = psi_ref[0, row], psi_ref[1, row]
        diag = cell(re, im, trap_ref[row])
        for f, field in enumerate((re, im, diag)):
            field_ref[f, row] = field
            moved = pltpu.roll(field, (8 * g + HALO) % 128, 1)
            packs[f][half] = jnp.where(group == g, moved, packs[f][half])
    first = lanes((depth, 128)) % 8 < HALO
    odd = is_odd(position()[1])
    for f in range(3):
        low, high = packs[f]
        to_right = jnp.where(first, low, pltpu.roll(high, HALO, 1))
        to_left = jnp.where(first, pltpu.roll(low, 128 - HALO, 1), high)
        s1_ref[f] = jnp.where(odd, to_left, to_right)
        s2_ref[f] = jnp.where(odd, to_right, to_left)


def merged(y1_ref, y2_ref, f, half):
    odd = is_odd(position()[1])
    first = lanes(y1_ref.shape[1:]) % 8 < HALO
    pole, poles = position()[1], lax.axis_size("pole")
    left = jnp.where(odd, y1_ref[f], y2_ref[f]) * (pole > 0).astype(jnp.float32)
    right = jnp.where(odd, y2_ref[f], y1_ref[f]) * (pole < poles - 1).astype(jnp.float32)
    if half:
        return jnp.where(first, pltpu.roll(left, 128 - HALO, 1), right)
    return jnp.where(first, left, pltpu.roll(right, HALO, 1))


def spread(pack, g):
    return pltpu.roll(pack, (128 - HALO - 8 * g) % 128, 1)


def cell(re, im, trap):
    return trap + COUPLING * (re * re + im * im) + DIAGONAL


def edge_items(high):
    skip = 1 if high else 0
    return [(f, i) for f in range(2) for i in range(HALO)] + [(2, skip + i) for i in range(HALO - 1)]


def end_kernel(psi_ref, trap_ref, s2_ref, s1_ref, raw, sems):
    rows = trap_ref.shape[0]
    copies = []
    for end in range(2):
        at = pl.ds((rows - HALO) * end, HALO)
        copies.append(pltpu.make_async_copy(psi_ref.at[:, at], raw.at[end, 0:2], sems.at[end, 0]))
        copies.append(pltpu.make_async_copy(trap_ref.at[at], raw.at[end, 2], sems.at[end, 1]))
    for copy in copies:
        copy.start()
    for copy in copies:
        copy.wait()
    even = jnp.logical_not(is_odd(position()[0]))
    for item, pair in enumerate(zip(edge_items(False), edge_items(True))):
        low, high = (
            raw[end, f, i] if f < 2 else cell(raw[end, 0, i], raw[end, 1, i], raw[end, 2, i])
            for end, (f, i) in enumerate(pair)
        )
        s1_ref[item] = jnp.where(even, high, low)
        s2_ref[item] = jnp.where(even, low, high)


def corner_kernel(x2_ref, x1_ref, corner_ref):
    items, depth = x1_ref.shape[:2]
    even = jnp.logical_not(is_odd(position()[0]))
    group = lanes((depth, 128)) // 8
    pack = jnp.zeros((depth, 128), jnp.float32)
    for high in (False, True):
        near, far = (x1_ref, x2_ref) if high else (x2_ref, x1_ref)
        for item in range(items):
            g = items + item if high else item
            moved = pltpu.roll(jnp.where(even, near[item], far[item]), (8 * g + HALO) % 128, 1)
            pack = jnp.where(group == g, moved, pack)
    corner_ref[...] = pack


def merged_corners(c1_ref, c2_ref):
    pole, poles = position()[1], lax.axis_size("pole")
    odd = is_odd(pole).astype(jnp.int32)
    first = lanes(c1_ref.shape) % 8 < HALO
    inside = jnp.where(first, (pole > 0).astype(jnp.float32), (pole < poles - 1).astype(jnp.float32))
    return jnp.where(first.astype(jnp.int32) == odd, c1_ref[...], c2_ref[...]) * inside


def neighbours_z(b):
    z = lax.broadcasted_iota(jnp.int32, (8, b.shape[1]), 0)
    low, high = b[0:8], b[8:16]
    low_up, high_up = pltpu.roll(low, 1, 0), pltpu.roll(high, 1, 0)
    low_down, high_down = pltpu.roll(low, 7, 0), pltpu.roll(high, 7, 0)
    return jnp.concatenate(
        [
            jnp.where(z == 0, 0.0, low_up) + jnp.where(z == 7, high_down, low_down),
            jnp.where(z == 0, low_up, high_up) + jnp.where(z == 7, 0.0, high_down),
        ],
        axis=0,
    )


def inside_mask(depth):
    pole, poles = position()[1], lax.axis_size("pole")
    lane = lanes((depth, 128))
    return jnp.where(lane < 64, (pole < poles - 1).astype(jnp.float32), (pole > 0).astype(jnp.float32))


def image(before, v, after, diag, inside):
    s = before + after
    p = (3.0 * K) * v + K * s
    e = 3.0 * p + (5.0 * K) * v
    w = e + neighbours_z(p)
    flat = diag * v + (14.0 * K) * s + neighbours_z(e)
    total = flat + pltpu.roll(w, 1, 1) + pltpu.roll(w, 255, 1)
    return jnp.concatenate([total[:, :128], total[:, 128:] * inside], axis=1)


def fold(a):
    return a[0:8, 0:128] + a[8:16, 0:128]


def forms(a, b):
    return fold(a[0] * b[0] - a[1] * b[1]), fold(a[0] * b[1] + a[1] * b[0])


def sweep(source, target, diag_ref, inside, reach):
    rows = source.shape[1]

    def step(i, sums):
        x = reach + i
        old = [source[c, x] for c in range(2)]
        new = [image(source[c, x - 1], old[c], source[c, x + 1], diag_ref[2, x], inside) for c in range(2)]
        if target is not None:
            for c in range(2):
                target[c, x] = new[c]
        return tuple(a + b for a, b in zip(sums, forms(old, old) + forms(old, new)))

    zero = jnp.zeros((8, 128), jnp.float32)
    return lax.fori_loop(0, rows - 2 * reach, step, (zero,) * 4, unroll=True)


def first_kernel(field_ref, y1_ref, y2_ref, grown_ref, u1_ref, sums_ref):
    rows, depth = field_ref.shape[1:3]
    for half in range(2):
        packs = [merged(y1_ref, y2_ref, f, half) for f in range(3)]
        for g in range(16):
            row = half * 16 + g
            for f in range(3):
                grown_ref[f, row, :, 0:128] = field_ref[f, row]
                grown_ref[f, row, :, 128:256] = spread(packs[f], g)
    inside = inside_mask(depth)
    sums = sweep(grown_ref, u1_ref, grown_ref, inside, 1)
    for j, part in enumerate(sums):
        sums_ref[j] = part


def second_kernel(grown_ref, u1_ref, u2_ref, sums_ref):
    inside = inside_mask(grown_ref.shape[2])
    sums = sweep(u1_ref, u2_ref, grown_ref, inside, 2) + sweep(u2_ref, None, grown_ref, inside, 3)
    for j, part in enumerate(sums):
        sums_ref[j] = part


def outer_kernel(
    shift_ref, weight_ref, grown_ref, u1_ref, u2_ref, sums1_ref, sums2_ref, x2_ref, x1_ref, c1_ref, c2_ref,
    b1_ref, b2_ref, line_ref,
):
    rows, depth = grown_ref.shape[1:3]
    tile, pole = position()
    tiles = lax.axis_size("tile")
    even = jnp.logical_not(is_odd(tile))
    inside = inside_mask(depth)
    sums = [ref[j] for ref in (sums1_ref, sums2_ref) for j in range(ref.shape[0])]
    corners = merged_corners(c1_ref, c2_ref)

    def count(j, parts):
        for i, part in enumerate(parts):
            sums[j + i] += part

    def end(high):
        own = (lambda i: rows - 1 + HALO - i) if high else (lambda i: i - HALO)
        there = (tile < tiles - 1) if high else (tile > 0)
        keep = jnp.where(there, inside, 0.0)
        keep = jnp.concatenate([jnp.broadcast_to(there.astype(jnp.float32), inside.shape), keep], axis=1)
        ones = jnp.concatenate([jnp.ones_like(inside), inside], axis=1)
        near, far = (x1_ref, x2_ref) if high else (x2_ref, x1_ref)
        v, diag = [{}, {}], {}
        items = edge_items(not high)
        for item, (f, i) in enumerate(items):
            side = spread(corners, len(items) + item if high else item)
            value = jnp.concatenate([jnp.where(even, near[item], far[item]), side], axis=1)
            place = HALO - 1 - i if high else i
            if f < 2:
                v[f][place] = value * there.astype(jnp.float32)
            else:
                diag[place] = value
        for i in range(HALO, 2 * HALO):
            for c in range(2):
                v[c][i] = grown_ref[c, own(i)]
            diag[i] = grown_ref[2, own(i)]

        def powers(source, first, last):
            return [
                {
                    i: image(source[c][i - 1], source[c][i], source[c][i + 1], diag[i], inside)
                    for i in range(first, last)
                }
                for c in range(2)
            ]

        def cut(found):
            for c in range(2):
                for i in found[c]:
                    if i < HALO:
                        found[c][i] = found[c][i] * keep
            return found

        def at(source, i):
            return [source[c][i] for c in range(2)]

        yield
        u1 = cut(powers(v, 1, HALO + 1))
        yield
        for c in range(2):
            for i in range(HALO + 1, HALO + 3):
                u1[c][i] = u1_ref[c, own(i)]
        u2 = cut(powers(u1, 2, HALO + 2))
        yield
        for c in range(2):
            for i in range(HALO + 2, HALO + 4):
                u2[c][i] = u2_ref[c, own(i)]
        u3 = powers(u2, HALO, HALO + 3)
        yield

        count(0, forms(at(v, HALO), at(v, HALO)))
        count(2, forms(at(v, HALO), at(u1, HALO)))
        for i in range(HALO, HALO + 2):
            count(4, forms(at(u1, i), at(u1, i)))
            count(6, forms(at(u1, i), at(u2, i)))
        for i in range(HALO, HALO + 3):
            count(8, forms(at(u2, i), at(u2, i)))
            count(10, forms(at(u2, i), at(u3, i)))
        for c in range(2):
            b1_ref[c, 1 if high else 0] = u1[c][HALO][:, 0:128]
            for i in range(2):
                b2_ref[c, 3 - i if high else i] = u2[c][HALO + i][:, 0:128]
        yield

    for _ in zip(end(False), end(True)):
        pass

    lane = lanes((1, 128))
    line = jnp.zeros((1, 128), jnp.float32)
    for j, part in enumerate(sums):
        line = jnp.where(lane == j, jnp.sum(part, keepdims=True), line)
    mine = shift_ref.shape[0]
    for i in range(mine):
        for c in range(2):
            for base, ref in ((SHIFT_LANE, shift_ref), (WEIGHT_LANE, weight_ref)):
                here = (lane == base + 16 * c + mine * pole + i) & (tile == 0)
                line = jnp.where(here, ref[i:i + 1, c:c + 1], line)
    line_ref[...] = jnp.broadcast_to(line, line_ref.shape)


def mul(a, b):
    return a[0] * b[0] - a[1] * b[1], a[0] * b[1] + a[1] * b[0]


def add(a, b):
    return a[0] + b[0], a[1] + b[1]


def sub(a, b):
    return a[0] - b[0], a[1] - b[1]


def over(a, b):
    norm = b[0] * b[0] + b[1] * b[1]
    factor = jnp.where(norm > 0.0, 1.0 / norm, 0.0)
    return (a[0] * b[0] + a[1] * b[1]) * factor, (a[1] * b[0] - a[0] * b[1]) * factor


def coefficients(line, poles):
    at = lanes((1, 128))

    def spot(j):
        return jnp.sum(jnp.where(at == j, line, 0.0), axis=1, keepdims=True) + jnp.zeros((1, 128), jnp.float32)

    m = [(spot(2 * j), spot(2 * j + 1)) for j in range(MOMENTS)]
    shift = tuple(pltpu.roll(line, (128 - SHIFT_LANE - 16 * c) % 128, 1) for c in range(2))
    weight = tuple(pltpu.roll(line, (128 - WEIGHT_LANE - 16 * c) % 128, 1) for c in range(2))
    scale = 1.0 / jnp.maximum(jnp.abs(m[0][0]), jnp.abs(m[0][1]))
    m = [(re * scale, im * scale) for re, im in m]
    mean = over(m[1], m[0])
    rest = list(m)
    for level in range(1, MOMENTS):
        for j in range(MOMENTS - 1, level - 1, -1):
            rest[j] = sub(rest[j], mul(mean, rest[j - 1]))
    c0, c2, c3, c4, c5 = rest[0], rest[2], rest[3], rest[4], rest[5]
    b1, e1 = over(c2, c0), over(c3, c2)
    d2 = sub(sub(c4, mul(e1, c3)), mul(b1, c2))
    b2 = over(d2, c2)
    e2 = over(sub(sub(sub(c5, mul(e1, c4)), mul(b1, c3)), mul(e1, d2)), d2)
    base = add((shift[1] / TIME_STEP + SIGMA, -shift[0] / TIME_STEP), mean)
    g2 = add(base, e2)
    g1 = sub(mul(add(base, e1), g2), b2)
    source = over((jnp.zeros_like(line), jnp.full_like(line, -1.0 / TIME_STEP)), sub(mul(base, g1), mul(b1, g2)))
    y0, y1, y2 = mul(source, g1), mul((-source[0], -source[1]), g2), source
    k1 = sub(y1, mul(e1, y2))
    k0 = sub(y0, mul(b1, y2))
    k0 = add(sub(k0, mul(mean, k1)), mul(mul(mean, mean), y2))
    twice = mul(mean, y2)
    k1 = sub(k1, (2.0 * twice[0], 2.0 * twice[1]))
    found = []
    for k in (k0, k1, y2):
        term = mul(weight, k)
        found.append(tuple(jnp.sum(jnp.where(at < poles, part, 0.0), axis=1, keepdims=True) for part in term))
    return found


def combine_kernel(poles, field_ref, u1_ref, u2_ref, b1_ref, b2_ref, sums_ref, out_ref, held, sems):
    line = jnp.sum(sums_ref[...], axis=0, keepdims=True)
    k = coefficients(line, poles)
    rows = field_ref.shape[1]
    k = [tuple(jnp.broadcast_to(part, (8, 128)) for part in pair) for pair in k]

    def source(inner, outer, reach, i):
        if i < reach:
            return outer, i
        if i >= rows - reach:
            return outer, i - rows + 2 * reach
        return inner, i

    parts = 2
    copies = []
    for i in range(rows):
        places = ((field_ref, i), source(u1_ref, b1_ref, 1, i), source(u2_ref, b2_ref, 2, i))
        for h in range(field_ref.shape[2] // 8):
            at = slice(8 * h, 8 * h + 8)
            total = None
            for pair, (ref, x) in zip(k, places):
                term = mul(pair, (ref[0, x, at, 0:128], ref[1, x, at, 0:128]))
                total = term if total is None else add(total, term)
            held[0, i, at] = total[0]
            held[1, i, at] = total[1]
        if (i + 1) % (rows // parts) == 0:
            part = pl.ds(i + 1 - rows // parts, rows // parts)
            for c in range(2):
                copy = pltpu.make_async_copy(held.at[c, part], out_ref.at[c, part], sems.at[c, len(copies) // 2])
                copy.start()
                copies.append(copy)
    for copy in copies:
        copy.wait()


def call(kernel, out_shape, specs, scratch=(), flops=0, bytes_accessed=0, aliases={}, out_spec=VMEM):
    return pl.pallas_call(
        kernel,
        out_shape=out_shape,
        in_specs=specs,
        out_specs=jax.tree.map(lambda _: out_spec, out_shape),
        scratch_shapes=list(scratch),
        input_output_aliases=aliases,
        compiler_params=pltpu.CompilerParams(vmem_limit_bytes=32 * 2**20),
        cost_estimate=pl.CostEstimate(flops=flops, bytes_accessed=bytes_accessed, transcendentals=0),
    )


def swaps(axis):
    size = lax.axis_size(axis)
    return [(i, i ^ 1) for i in range(size)], [(i, (i + 1 - 2 * (i % 2 == 0)) % size) for i in range(size)]


def on_device(psi, trap, pole_shift, pole_weight):
    tiles, poles = lax.axis_size("tile"), lax.axis_size("pole")
    rows, depth, width = trap.shape
    f32 = functools.partial(jax.ShapeDtypeStruct, dtype=jnp.float32)

    edge = f32((3 * HALO - 1, depth, width))
    s2, s1 = call(
        end_kernel, (edge, edge), [ANYWHERE] * 2,
        [pltpu.VMEM((2, 3, HALO, depth, width), jnp.float32), pltpu.SemaphoreType.DMA((2, 2))],
        flops=2_000_000_000, bytes_accessed=40_000_000,
    )(*(pltpu.with_memory_space_constraint(x, pltpu.HBM) for x in (psi, trap)))
    near, across = swaps("tile")
    pairs = []
    for pole in range(poles):
        for tile, other in across:
            pairs.append((pole * tiles + tile, (pole * tiles + other) if abs(tile - other) == 1 else ((pole ^ 1) * tiles + tile)))
    x2 = lax.ppermute(s2, ("pole", "tile"), pairs)
    x1 = lax.ppermute(s1, "tile", near)

    message = f32((3, depth, 128))
    m1, m2, field = call(
        load_kernel, (message, message, f32((3, rows, depth, width))), [VMEM] * 2,
    )(psi, trap)
    pole_near, pole_across = swaps("pole")
    sides = []
    for pole, other in pole_across:
        for tile in range(tiles):
            sides.append((pole * tiles + tile, (other * tiles + tile) if abs(pole - other) == 1 else (pole * tiles + (tile ^ 1))))
    y2 = lax.ppermute(m2, ("pole", "tile"), sides)
    y1 = lax.ppermute(m1, "pole", pole_near)

    wide = f32((2, rows, depth, 2 * width))
    grown, u1, sums1 = call(
        first_kernel,
        (f32((3, rows, depth, 2 * width)), wide, f32((4, 8, 128))),
        [VMEM] * 3, flops=8_000_000, bytes_accessed=3_000_000,
    )(field, y1, y2)
    x2, x1, sums1 = lax.optimization_barrier((x2, x1, sums1))
    corner = call(corner_kernel, f32((depth, 128)), [VMEM] * 2)(x2, x1)
    c2 = lax.ppermute(corner, ("pole", "tile"), sides)
    c1 = lax.ppermute(corner, "pole", pole_near)

    u2, sums2 = call(
        second_kernel, (wide, f32((8, 8, 128))), [VMEM] * 2, flops=12_000_000, bytes_accessed=5_000_000,
    )(grown, u1)

    devices = tiles * poles
    b1, b2, line = call(
        outer_kernel,
        (f32((2, 2, depth, width)), f32((2, 4, depth, width)), f32((devices, 128))),
        [VMEM] * 11,
    )(pole_shift, pole_weight, grown, u1, u2, sums1, sums2, x2, x1, c1, c2)

    lines = lax.all_to_all(line.reshape(devices, 1, 128), ("pole", "tile"), 0, 0, tiled=True)
    combine = functools.partial(combine_kernel, pole_shift.shape[0] * poles)
    return call(
        combine, f32((2, rows, depth, width)), [VMEM] * 6,
        [pltpu.VMEM((2, rows, depth, width), jnp.float32), pltpu.SemaphoreType.DMA((2, 2))], out_spec=ANYWHERE,
    )(field, u1, u2, b1, b2, lines.reshape(devices, 128))


def solution(mesh):
    placed = (
        P(None, "tile", None, "pole"),
        P("tile", None, "pole"),
        P("pole", None),
        P("pole", None),
    )
    return jax.shard_map(
        on_device,
        mesh=mesh,
        in_specs=placed,
        out_specs=P(None, "tile", None, "pole"),
        check_vma=False,
    )
```

```python
import functools

import jax
import jax.numpy as jnp
from jax import lax
from jax.experimental import pallas as pl
from jax.experimental.pallas import tpu as pltpu
from jax.sharding import PartitionSpec as P

COUPLING = 0.5
TIME_STEP = 0.25
SIGMA = 3.0
HALO = 3
K = -0.5 / 30.0
DIAGONAL = -128.0 * K - SIGMA
MOMENTS = 6
SHIFT_LANE, WEIGHT_LANE = 16, 48
VMEM = pl.BlockSpec(memory_space=pltpu.VMEM)
ANYWHERE = pl.BlockSpec(memory_space=pl.ANY)


def lanes(shape):
    return lax.broadcasted_iota(jnp.int32, shape, len(shape) - 1)


def position():
    return lax.axis_index("tile"), lax.axis_index("pole")


def is_odd(index):
    return lax.rem(index, 2) == 1


def load_kernel(psi_ref, trap_ref, s1_ref, s2_ref, field_ref):
    rows, depth = trap_ref.shape[:2]
    half_rows = rows // 2
    group = lanes((depth, 128)) // 8
    packs = [[jnp.zeros((depth, 128), jnp.float32)] * 2 for _ in range(3)]
    for row in range(rows):
        half, g = divmod(row, half_rows)
        re, im = psi_ref[0, row], psi_ref[1, row]
        diag = cell(re, im, trap_ref[row])
        for f, field in enumerate((re, im, diag)):
            field_ref[f, row] = field
            moved = pltpu.roll(field, (8 * g + HALO) % 128, 1)
            packs[f][half] = jnp.where(group == g, moved, packs[f][half])
    first = lanes((depth, 128)) % 8 < HALO
    odd = is_odd(position()[1])
    for f in range(3):
        low, high = packs[f]
        to_right = jnp.where(first, low, pltpu.roll(high, HALO, 1))
        to_left = jnp.where(first, pltpu.roll(low, 128 - HALO, 1), high)
        s1_ref[f] = jnp.where(odd, to_left, to_right)
        s2_ref[f] = jnp.where(odd, to_right, to_left)


def merged(y1_ref, y2_ref, f, half):
    odd = is_odd(position()[1])
    first = lanes(y1_ref.shape[1:]) % 8 < HALO
    pole, poles = position()[1], lax.axis_size("pole")
    left = jnp.where(odd, y1_ref[f], y2_ref[f]) * (pole > 0).astype(jnp.float32)
    right = jnp.where(odd, y2_ref[f], y1_ref[f]) * (pole < poles - 1).astype(jnp.float32)
    if half:
        return jnp.where(first, pltpu.roll(left, 128 - HALO, 1), right)
    return jnp.where(first, left, pltpu.roll(right, HALO, 1))


def spread(pack, g):
    return pltpu.roll(pack, (128 - HALO - 8 * g) % 128, 1)


def cell(re, im, trap):
    return trap + COUPLING * (re * re + im * im) + DIAGONAL


def edge_items(high):
    skip = 1 if high else 0
    return [(f, i) for f in range(2) for i in range(HALO)] + [(2, skip + i) for i in range(HALO - 1)]


def end_kernel(psi_ref, trap_ref, s2_ref, s1_ref, raw, sems):
    rows = trap_ref.shape[0]
    copies = []
    for end in range(2):
        at = pl.ds((rows - HALO) * end, HALO)
        copies.append(pltpu.make_async_copy(psi_ref.at[:, at], raw.at[end, 0:2], sems.at[end, 0]))
        copies.append(pltpu.make_async_copy(trap_ref.at[at], raw.at[end, 2], sems.at[end, 1]))
    for copy in copies:
        copy.start()
    for copy in copies:
        copy.wait()
    even = jnp.logical_not(is_odd(position()[0]))
    for item, pair in enumerate(zip(edge_items(False), edge_items(True))):
        low, high = (
            raw[end, f, i] if f < 2 else cell(raw[end, 0, i], raw[end, 1, i], raw[end, 2, i])
            for end, (f, i) in enumerate(pair)
        )
        s1_ref[item] = jnp.where(even, high, low)
        s2_ref[item] = jnp.where(even, low, high)


def corner_kernel(x2_ref, x1_ref, corner_ref):
    items, depth = x1_ref.shape[:2]
    even = jnp.logical_not(is_odd(position()[0]))
    group = lanes((depth, 128)) // 8
    pack = jnp.zeros((depth, 128), jnp.float32)
    for high in (False, True):
        near, far = (x1_ref, x2_ref) if high else (x2_ref, x1_ref)
        for item in range(items):
            g = items + item if high else item
            moved = pltpu.roll(jnp.where(even, near[item], far[item]), (8 * g + HALO) % 128, 1)
            pack = jnp.where(group == g, moved, pack)
    corner_ref[...] = pack


def merged_corners(c1_ref, c2_ref):
    pole, poles = position()[1], lax.axis_size("pole")
    odd = is_odd(pole).astype(jnp.int32)
    first = lanes(c1_ref.shape) % 8 < HALO
    inside = jnp.where(first, (pole > 0).astype(jnp.float32), (pole < poles - 1).astype(jnp.float32))
    return jnp.where(first.astype(jnp.int32) == odd, c1_ref[...], c2_ref[...]) * inside


def neighbours_z(b):
    z = lax.broadcasted_iota(jnp.int32, (8, b.shape[1]), 0)
    low, high = b[0:8], b[8:16]
    low_up, high_up = pltpu.roll(low, 1, 0), pltpu.roll(high, 1, 0)
    low_down, high_down = pltpu.roll(low, 7, 0), pltpu.roll(high, 7, 0)
    return jnp.concatenate(
        [
            jnp.where(z == 0, 0.0, low_up) + jnp.where(z == 7, high_down, low_down),
            jnp.where(z == 0, low_up, high_up) + jnp.where(z == 7, 0.0, high_down),
        ],
        axis=0,
    )


def inside_mask(depth):
    pole, poles = position()[1], lax.axis_size("pole")
    lane = lanes((depth, 128))
    return jnp.where(lane < 64, (pole < poles - 1).astype(jnp.float32), (pole > 0).astype(jnp.float32))


def image(before, v, after, diag, inside):
    s = before + after
    p = (3.0 * K) * v + K * s
    e = 3.0 * p + (5.0 * K) * v
    w = e + neighbours_z(p)
    flat = diag * v + (14.0 * K) * s + neighbours_z(e)
    total = flat + pltpu.roll(w, 1, 1) + pltpu.roll(w, 255, 1)
    return jnp.concatenate([total[:, :128], total[:, 128:] * inside], axis=1)


def fold(a):
    return a[0:8, 0:128] + a[8:16, 0:128]


def forms(a, b):
    return fold(a[0] * b[0] - a[1] * b[1]), fold(a[0] * b[1] + a[1] * b[0])


def sweep(source, target, diag_ref, inside, reach):
    rows = source.shape[1]

    def step(i, sums):
        x = reach + i
        old = [source[c, x] for c in range(2)]
        new = [image(source[c, x - 1], old[c], source[c, x + 1], diag_ref[2, x], inside) for c in range(2)]
        if target is not None:
            for c in range(2):
                target[c, x] = new[c]
        return tuple(a + b for a, b in zip(sums, forms(old, old) + forms(old, new)))

    zero = jnp.zeros((8, 128), jnp.float32)
    return lax.fori_loop(0, rows - 2 * reach, step, (zero,) * 4, unroll=True)


def first_kernel(field_ref, y1_ref, y2_ref, grown_ref, u1_ref, sums_ref):
    rows, depth = field_ref.shape[1:3]
    for half in range(2):
        packs = [merged(y1_ref, y2_ref, f, half) for f in range(3)]
        for g in range(16):
            row = half * 16 + g
            for f in range(3):
                grown_ref[f, row, :, 0:128] = field_ref[f, row]
                grown_ref[f, row, :, 128:256] = spread(packs[f], g)
    inside = inside_mask(depth)
    sums = sweep(grown_ref, u1_ref, grown_ref, inside, 1)
    for j, part in enumerate(sums):
        sums_ref[j] = part


def second_kernel(grown_ref, u1_ref, u2_ref, sums_ref):
    inside = inside_mask(grown_ref.shape[2])
    sums = sweep(u1_ref, u2_ref, grown_ref, inside, 2) + sweep(u2_ref, None, grown_ref, inside, 3)
    for j, part in enumerate(sums):
        sums_ref[j] = part


def outer_kernel(
    shift_ref, weight_ref, grown_ref, u1_ref, u2_ref, sums1_ref, sums2_ref, x2_ref, x1_ref, c2_ref, c1_ref,
    b1_ref, b2_ref, line_ref,
):
    rows, depth = grown_ref.shape[1:3]
    tile, pole = position()
    tiles = lax.axis_size("tile")
    even = jnp.logical_not(is_odd(tile))
    inside = inside_mask(depth)
    sums = [ref[j] for ref in (sums1_ref, sums2_ref) for j in range(ref.shape[0])]
    corners = merged_corners(c1_ref, c2_ref)

    def count(j, parts):
        for i, part in enumerate(parts):
            sums[j + i] += part

    def end(high):
        own = (lambda i: rows - 1 + HALO - i) if high else (lambda i: i - HALO)
        there = (tile < tiles - 1) if high else (tile > 0)
        keep = jnp.where(there, inside, 0.0)
        keep = jnp.concatenate([jnp.broadcast_to(there.astype(jnp.float32), inside.shape), keep], axis=1)
        ones = jnp.concatenate([jnp.ones_like(inside), inside], axis=1)
        near, far = (x1_ref, x2_ref) if high else (x2_ref, x1_ref)
        v, diag = [{}, {}], {}
        items = edge_items(not high)
        for item, (f, i) in enumerate(items):
            side = spread(corners, len(items) + item if high else item)
            value = jnp.concatenate([jnp.where(even, near[item], far[item]), side], axis=1)
            place = HALO - 1 - i if high else i
            if f < 2:
                v[f][place] = value * there.astype(jnp.float32)
            else:
                diag[place] = value
        for i in range(HALO, 2 * HALO):
            for c in range(2):
                v[c][i] = grown_ref[c, own(i)]
            diag[i] = grown_ref[2, own(i)]

        def powers(source, first, last):
            return [
                {
                    i: image(source[c][i - 1], source[c][i], source[c][i + 1], diag[i], inside)
                    for i in range(first, last)
                }
                for c in range(2)
            ]

        def cut(found):
            for c in range(2):
                for i in found[c]:
                    if i < HALO:
                        found[c][i] = found[c][i] * keep
            return found

        def at(source, i):
            return [source[c][i] for c in range(2)]

        yield
        u1 = cut(powers(v, 1, HALO + 1))
        yield
        for c in range(2):
            for i in range(HALO + 1, HALO + 3):
                u1[c][i] = u1_ref[c, own(i)]
        u2 = cut(powers(u1, 2, HALO + 2))
        yield
        for c in range(2):
            for i in range(HALO + 2, HALO + 4):
                u2[c][i] = u2_ref[c, own(i)]
        u3 = powers(u2, HALO, HALO + 3)
        yield

        count(0, forms(at(v, HALO), at(v, HALO)))
        count(2, forms(at(v, HALO), at(u1, HALO)))
        for i in range(HALO, HALO + 2):
            count(4, forms(at(u1, i), at(u1, i)))
            count(6, forms(at(u1, i), at(u2, i)))
        for i in range(HALO, HALO + 3):
            count(8, forms(at(u2, i), at(u2, i)))
            count(10, forms(at(u2, i), at(u3, i)))
        for c in range(2):
            b1_ref[c, 1 if high else 0] = u1[c][HALO][:, 0:128]
            for i in range(2):
                b2_ref[c, 3 - i if high else i] = u2[c][HALO + i][:, 0:128]
        yield

    for _ in zip(end(False), end(True)):
        pass

    lane = lanes((1, 128))
    line = jnp.zeros((1, 128), jnp.float32)
    for j, part in enumerate(sums):
        line = jnp.where(lane == j, jnp.sum(part, keepdims=True), line)
    mine = shift_ref.shape[0]
    for i in range(mine):
        for c in range(2):
            for base, ref in ((SHIFT_LANE, shift_ref), (WEIGHT_LANE, weight_ref)):
                here = (lane == base + 16 * c + mine * pole + i) & (tile == 0)
                line = jnp.where(here, ref[i:i + 1, c:c + 1], line)
    line_ref[...] = jnp.broadcast_to(line, line_ref.shape)


def mul(a, b):
    return a[0] * b[0] - a[1] * b[1], a[0] * b[1] + a[1] * b[0]


def add(a, b):
    return a[0] + b[0], a[1] + b[1]


def sub(a, b):
    return a[0] - b[0], a[1] - b[1]


def over(a, b):
    norm = b[0] * b[0] + b[1] * b[1]
    factor = jnp.where(norm > 0.0, 1.0 / norm, 0.0)
    return (a[0] * b[0] + a[1] * b[1]) * factor, (a[1] * b[0] - a[0] * b[1]) * factor


def coefficients(line, poles):
    at = lanes((1, 128))

    def spot(j):
        return jnp.sum(jnp.where(at == j, line, 0.0), axis=1, keepdims=True) + jnp.zeros((1, 128), jnp.float32)

    m = [(spot(2 * j), spot(2 * j + 1)) for j in range(MOMENTS)]
    shift = tuple(pltpu.roll(line, (128 - SHIFT_LANE - 16 * c) % 128, 1) for c in range(2))
    weight = tuple(pltpu.roll(line, (128 - WEIGHT_LANE - 16 * c) % 128, 1) for c in range(2))
    scale = 1.0 / jnp.maximum(jnp.abs(m[0][0]), jnp.abs(m[0][1]))
    m = [(re * scale, im * scale) for re, im in m]
    mean = over(m[1], m[0])
    rest = list(m)
    for level in range(1, MOMENTS):
        for j in range(MOMENTS - 1, level - 1, -1):
            rest[j] = sub(rest[j], mul(mean, rest[j - 1]))
    c0, c2, c3, c4, c5 = rest[0], rest[2], rest[3], rest[4], rest[5]
    b1, e1 = over(c2, c0), over(c3, c2)
    d2 = sub(sub(c4, mul(e1, c3)), mul(b1, c2))
    b2 = over(d2, c2)
    e2 = over(sub(sub(sub(c5, mul(e1, c4)), mul(b1, c3)), mul(e1, d2)), d2)
    base = add((shift[1] / TIME_STEP + SIGMA, -shift[0] / TIME_STEP), mean)
    g2 = add(base, e2)
    g1 = sub(mul(add(base, e1), g2), b2)
    source = over((jnp.zeros_like(line), jnp.full_like(line, -1.0 / TIME_STEP)), sub(mul(base, g1), mul(b1, g2)))
    y0, y1, y2 = mul(source, g1), mul((-source[0], -source[1]), g2), source
    k1 = sub(y1, mul(e1, y2))
    k0 = sub(y0, mul(b1, y2))
    k0 = add(sub(k0, mul(mean, k1)), mul(mul(mean, mean), y2))
    twice = mul(mean, y2)
    k1 = sub(k1, (2.0 * twice[0], 2.0 * twice[1]))
    found = []
    for k in (k0, k1, y2):
        term = mul(weight, k)
        found.append(tuple(jnp.sum(jnp.where(at < poles, part, 0.0), axis=1, keepdims=True) for part in term))
    return found


def combine_kernel(poles, field_ref, u1_ref, u2_ref, b1_ref, b2_ref, sums_ref, out_ref, held, sems):
    line = jnp.sum(sums_ref[...], axis=0, keepdims=True)
    k = coefficients(line, poles)
    rows = field_ref.shape[1]
    k = [tuple(jnp.broadcast_to(part, (8, 128)) for part in pair) for pair in k]

    def source(inner, outer, reach, i):
        if i < reach:
            return outer, i
        if i >= rows - reach:
            return outer, i - rows + 2 * reach
        return inner, i

    parts = 2
    copies = []
    for i in range(rows):
        places = ((field_ref, i), source(u1_ref, b1_ref, 1, i), source(u2_ref, b2_ref, 2, i))
        for h in range(field_ref.shape[2] // 8):
            at = slice(8 * h, 8 * h + 8)
            total = None
            for pair, (ref, x) in zip(k, places):
                term = mul(pair, (ref[0, x, at, 0:128], ref[1, x, at, 0:128]))
                total = term if total is None else add(total, term)
            held[0, i, at] = total[0]
            held[1, i, at] = total[1]
        if (i + 1) % (rows // parts) == 0:
            part = pl.ds(i + 1 - rows // parts, rows // parts)
            for c in range(2):
                copy = pltpu.make_async_copy(held.at[c, part], out_ref.at[c, part], sems.at[c, len(copies) // 2])
                copy.start()
                copies.append(copy)
    for copy in copies:
        copy.wait()


def call(kernel, out_shape, specs, scratch=(), flops=0, bytes_accessed=0, aliases={}, out_spec=VMEM):
    return pl.pallas_call(
        kernel,
        out_shape=out_shape,
        in_specs=specs,
        out_specs=jax.tree.map(lambda _: out_spec, out_shape),
        scratch_shapes=list(scratch),
        input_output_aliases=aliases,
        compiler_params=pltpu.CompilerParams(vmem_limit_bytes=32 * 2**20),
        cost_estimate=pl.CostEstimate(flops=flops, bytes_accessed=bytes_accessed, transcendentals=0),
    )


def swaps(axis):
    size = lax.axis_size(axis)
    return [(i, i ^ 1) for i in range(size)], [(i, (i + 1 - 2 * (i % 2 == 0)) % size) for i in range(size)]


def on_device(psi, trap, pole_shift, pole_weight):
    tiles, poles = lax.axis_size("tile"), lax.axis_size("pole")
    rows, depth, width = trap.shape
    f32 = functools.partial(jax.ShapeDtypeStruct, dtype=jnp.float32)

    edge = f32((3 * HALO - 1, depth, width))
    s2, s1 = call(
        end_kernel, (edge, edge), [ANYWHERE] * 2,
        [pltpu.VMEM((2, 3, HALO, depth, width), jnp.float32), pltpu.SemaphoreType.DMA((2, 2))],
        flops=2_000_000_000, bytes_accessed=40_000_000,
    )(*(pltpu.with_memory_space_constraint(x, pltpu.HBM) for x in (psi, trap)))
    near, across = swaps("tile")
    pairs = []
    for pole in range(poles):
        for tile, other in across:
            pairs.append((pole * tiles + tile, (pole * tiles + other) if abs(tile - other) == 1 else ((pole ^ 1) * tiles + tile)))
    x2 = lax.ppermute(s2, ("pole", "tile"), pairs)
    x1 = lax.ppermute(s1, "tile", near)

    message = f32((3, depth, 128))
    m1, m2, field = call(
        load_kernel, (message, message, f32((3, rows, depth, width))), [VMEM] * 2,
    )(psi, trap)
    pole_near, pole_across = swaps("pole")
    y2 = lax.ppermute(m2, "pole", pole_across)
    y1 = lax.ppermute(m1, "pole", pole_near)

    wide = f32((2, rows, depth, 2 * width))
    grown, u1, sums1 = call(
        first_kernel,
        (f32((3, rows, depth, 2 * width)), wide, f32((4, 8, 128))),
        [VMEM] * 3, flops=8_000_000, bytes_accessed=3_000_000,
    )(field, y1, y2)
    x2, x1, sums1 = lax.optimization_barrier((x2, x1, sums1))
    corner = call(corner_kernel, f32((depth, 128)), [VMEM] * 2)(x2, x1)
    c2 = lax.ppermute(corner, "pole", pole_across)
    c1 = lax.ppermute(corner, "pole", pole_near)

    u2, sums2 = call(
        second_kernel, (wide, f32((8, 8, 128))), [VMEM] * 2, flops=12_000_000, bytes_accessed=5_000_000,
    )(grown, u1)

    devices = tiles * poles
    b1, b2, line = call(
        outer_kernel,
        (f32((2, 2, depth, width)), f32((2, 4, depth, width)), f32((devices, 128))),
        [VMEM] * 11,
    )(pole_shift, pole_weight, grown, u1, u2, sums1, sums2, x2, x1, c2, c1)

    lines = lax.all_to_all(line.reshape(devices, 1, 128), ("pole", "tile"), 0, 0, tiled=True)
    combine = functools.partial(combine_kernel, pole_shift.shape[0] * poles)
    return call(
        combine, f32((2, rows, depth, width)), [VMEM] * 6,
        [pltpu.VMEM((2, rows, depth, width), jnp.float32), pltpu.SemaphoreType.DMA((2, 2))], out_spec=ANYWHERE,
    )(field, u1, u2, b1, b2, lines.reshape(devices, 128))


def solution(mesh):
    placed = (
        P(None, "tile", None, "pole"),
        P("tile", None, "pole"),
        P("pole", None),
        P("pole", None),
    )
    return jax.shard_map(
        on_device,
        mesh=mesh,
        in_specs=placed,
        out_specs=P(None, "tile", None, "pole"),
        check_vma=False,
    )
```

```python
import functools

import jax
import jax.numpy as jnp
from jax import lax
from jax.experimental import pallas as pl
from jax.experimental.pallas import tpu as pltpu
from jax.sharding import PartitionSpec as P

COUPLING = 0.5
TIME_STEP = 0.25
SIGMA = 3.0
HALO = 3
K = -0.5 / 30.0
DIAGONAL = -128.0 * K - SIGMA
MOMENTS = 6
SHIFT_LANE, WEIGHT_LANE = 16, 48
VMEM = pl.BlockSpec(memory_space=pltpu.VMEM)
ANYWHERE = pl.BlockSpec(memory_space=pl.ANY)


def lanes(shape):
    return lax.broadcasted_iota(jnp.int32, shape, len(shape) - 1)


def position():
    return lax.axis_index("tile"), lax.axis_index("pole")


def is_odd(index):
    return lax.rem(index, 2) == 1


def load_kernel(psi_ref, trap_ref, s1_ref, s2_ref, field_ref):
    rows, depth = trap_ref.shape[:2]
    half_rows = rows // 2
    group = lanes((depth, 128)) // 8
    packs = [[jnp.zeros((depth, 128), jnp.float32)] * 2 for _ in range(3)]
    for row in range(rows):
        half, g = divmod(row, half_rows)
        re, im = psi_ref[0, row], psi_ref[1, row]
        diag = cell(re, im, trap_ref[row])
        for f, field in enumerate((re, im, diag)):
            field_ref[f, row] = field
            moved = pltpu.roll(field, (8 * g + HALO) % 128, 1)
            packs[f][half] = jnp.where(group == g, moved, packs[f][half])
    first = lanes((depth, 128)) % 8 < HALO
    odd = is_odd(position()[1])
    for f in range(3):
        low, high = packs[f]
        to_right = jnp.where(first, low, pltpu.roll(high, HALO, 1))
        to_left = jnp.where(first, pltpu.roll(low, 128 - HALO, 1), high)
        s1_ref[f] = jnp.where(odd, to_left, to_right)
        s2_ref[f] = jnp.where(odd, to_right, to_left)


def merged(y1_ref, y2_ref, f, half):
    odd = is_odd(position()[1])
    first = lanes(y1_ref.shape[1:]) % 8 < HALO
    pole, poles = position()[1], lax.axis_size("pole")
    left = jnp.where(odd, y1_ref[f], y2_ref[f]) * (pole > 0).astype(jnp.float32)
    right = jnp.where(odd, y2_ref[f], y1_ref[f]) * (pole < poles - 1).astype(jnp.float32)
    if half:
        return jnp.where(first, pltpu.roll(left, 128 - HALO, 1), right)
    return jnp.where(first, left, pltpu.roll(right, HALO, 1))


def spread(pack, g):
    return pltpu.roll(pack, (128 - HALO - 8 * g) % 128, 1)


def cell(re, im, trap):
    return trap + COUPLING * (re * re + im * im) + DIAGONAL


def edge_items(high):
    skip = 1 if high else 0
    return [(f, i) for f in range(2) for i in range(HALO)] + [(2, skip + i) for i in range(HALO - 1)]


def end_kernel(psi_ref, trap_ref, s2_ref, s1_ref, raw, sems):
    rows = trap_ref.shape[0]
    copies = []
    for end in range(2):
        at = pl.ds((rows - HALO) * end, HALO)
        copies.append(pltpu.make_async_copy(psi_ref.at[:, at], raw.at[end, 0:2], sems.at[end, 0]))
        copies.append(pltpu.make_async_copy(trap_ref.at[at], raw.at[end, 2], sems.at[end, 1]))
    for copy in copies:
        copy.start()
    for copy in copies:
        copy.wait()
    even = jnp.logical_not(is_odd(position()[0]))
    for item, pair in enumerate(zip(edge_items(False), edge_items(True))):
        low, high = (
            raw[end, f, i] if f < 2 else cell(raw[end, 0, i], raw[end, 1, i], raw[end, 2, i])
            for end, (f, i) in enumerate(pair)
        )
        s1_ref[item] = jnp.where(even, high, low)
        s2_ref[item] = jnp.where(even, low, high)


def corner_kernel(x2_ref, x1_ref, corner_ref):
    items, depth = x1_ref.shape[:2]
    even = jnp.logical_not(is_odd(position()[0]))
    group = lanes((depth, 128)) // 8
    pack = jnp.zeros((depth, 128), jnp.float32)
    for high in (False, True):
        near, far = (x1_ref, x2_ref) if high else (x2_ref, x1_ref)
        for item in range(items):
            g = items + item if high else item
            moved = pltpu.roll(jnp.where(even, near[item], far[item]), (8 * g + HALO) % 128, 1)
            pack = jnp.where(group == g, moved, pack)
    corner_ref[...] = pack


def merged_corners(c1_ref, c2_ref):
    pole, poles = position()[1], lax.axis_size("pole")
    odd = is_odd(pole).astype(jnp.int32)
    first = lanes(c1_ref.shape) % 8 < HALO
    inside = jnp.where(first, (pole > 0).astype(jnp.float32), (pole < poles - 1).astype(jnp.float32))
    return jnp.where(first.astype(jnp.int32) == odd, c1_ref[...], c2_ref[...]) * inside


def neighbours_z(b):
    z = lax.broadcasted_iota(jnp.int32, (8, b.shape[1]), 0)
    low, high = b[0:8], b[8:16]
    low_up, high_up = pltpu.roll(low, 1, 0), pltpu.roll(high, 1, 0)
    low_down, high_down = pltpu.roll(low, 7, 0), pltpu.roll(high, 7, 0)
    return jnp.concatenate(
        [
            jnp.where(z == 0, 0.0, low_up) + jnp.where(z == 7, high_down, low_down),
            jnp.where(z == 0, low_up, high_up) + jnp.where(z == 7, 0.0, high_down),
        ],
        axis=0,
    )


def inside_mask(depth):
    pole, poles = position()[1], lax.axis_size("pole")
    lane = lanes((depth, 128))
    return jnp.where(lane < 64, (pole < poles - 1).astype(jnp.float32), (pole > 0).astype(jnp.float32))


def image(before, v, after, diag, inside):
    s = before + after
    p = (3.0 * K) * v + K * s
    e = 3.0 * p + (5.0 * K) * v
    w = e + neighbours_z(p)
    flat = diag * v + (14.0 * K) * s + neighbours_z(e)
    total = flat + pltpu.roll(w, 1, 1) + pltpu.roll(w, 255, 1)
    return jnp.concatenate([total[:, :128], total[:, 128:] * inside], axis=1)


def fold(a):
    return a[0:8, 0:128] + a[8:16, 0:128]


def forms(a, b):
    return fold(a[0] * b[0] - a[1] * b[1]), fold(a[0] * b[1] + a[1] * b[0])


def sweep(source, target, diag_ref, inside, reach):
    rows = source.shape[1]

    def step(i, sums):
        x = reach + i
        old = [source[c, x] for c in range(2)]
        new = [image(source[c, x - 1], old[c], source[c, x + 1], diag_ref[2, x], inside) for c in range(2)]
        if target is not None:
            for c in range(2):
                target[c, x] = new[c]
        return tuple(a + b for a, b in zip(sums, forms(old, old) + forms(old, new)))

    zero = jnp.zeros((8, 128), jnp.float32)
    return lax.fori_loop(0, rows - 2 * reach, step, (zero,) * 4, unroll=True)


def first_kernel(field_ref, y1_ref, y2_ref, grown_ref, u1_ref, sums_ref):
    rows, depth = field_ref.shape[1:3]
    for half in range(2):
        packs = [merged(y1_ref, y2_ref, f, half) for f in range(3)]
        for g in range(16):
            row = half * 16 + g
            for f in range(3):
                grown_ref[f, row, :, 0:128] = field_ref[f, row]
                grown_ref[f, row, :, 128:256] = spread(packs[f], g)
    inside = inside_mask(depth)
    sums = sweep(grown_ref, u1_ref, grown_ref, inside, 1)
    for j, part in enumerate(sums):
        sums_ref[j] = part


def second_kernel(grown_ref, u1_ref, u2_ref, sums_ref):
    inside = inside_mask(grown_ref.shape[2])
    sums = sweep(u1_ref, u2_ref, grown_ref, inside, 2) + sweep(u2_ref, None, grown_ref, inside, 3)
    for j, part in enumerate(sums):
        sums_ref[j] = part


def outer_kernel(
    shift_ref, weight_ref, grown_ref, u1_ref, u2_ref, sums1_ref, sums2_ref, x2_ref, x1_ref, c1_ref, c2_ref,
    b1_ref, b2_ref, line_ref,
):
    rows, depth = grown_ref.shape[1:3]
    tile, pole = position()
    tiles = lax.axis_size("tile")
    even = jnp.logical_not(is_odd(tile))
    inside = inside_mask(depth)
    sums = [ref[j] for ref in (sums1_ref, sums2_ref) for j in range(ref.shape[0])]
    corners = merged_corners(c1_ref, c2_ref)

    def count(j, parts):
        for i, part in enumerate(parts):
            sums[j + i] += part

    def end(high):
        own = (lambda i: rows - 1 + HALO - i) if high else (lambda i: i - HALO)
        there = (tile < tiles - 1) if high else (tile > 0)
        keep = jnp.where(there, inside, 0.0)
        keep = jnp.concatenate([jnp.broadcast_to(there.astype(jnp.float32), inside.shape), keep], axis=1)
        ones = jnp.concatenate([jnp.ones_like(inside), inside], axis=1)
        near, far = (x1_ref, x2_ref) if high else (x2_ref, x1_ref)
        v, diag = [{}, {}], {}
        items = edge_items(not high)
        for item, (f, i) in enumerate(items):
            side = spread(corners, len(items) + item if high else item)
            value = jnp.concatenate([jnp.where(even, near[item], far[item]), side], axis=1)
            place = HALO - 1 - i if high else i
            if f < 2:
                v[f][place] = value * there.astype(jnp.float32)
            else:
                diag[place] = value
        for i in range(HALO, 2 * HALO):
            for c in range(2):
                v[c][i] = grown_ref[c, own(i)]
            diag[i] = grown_ref[2, own(i)]

        def powers(source, first, last):
            return [
                {
                    i: image(source[c][i - 1], source[c][i], source[c][i + 1], diag[i], inside)
                    for i in range(first, last)
                }
                for c in range(2)
            ]

        def cut(found):
            for c in range(2):
                for i in found[c]:
                    if i < HALO:
                        found[c][i] = found[c][i] * keep
            return found

        def at(source, i):
            return [source[c][i] for c in range(2)]

        yield
        u1 = cut(powers(v, 1, HALO + 1))
        yield
        for c in range(2):
            for i in range(HALO + 1, HALO + 3):
                u1[c][i] = u1_ref[c, own(i)]
        u2 = cut(powers(u1, 2, HALO + 2))
        yield
        for c in range(2):
            for i in range(HALO + 2, HALO + 4):
                u2[c][i] = u2_ref[c, own(i)]
        u3 = powers(u2, HALO, HALO + 3)
        yield

        count(0, forms(at(v, HALO), at(v, HALO)))
        count(2, forms(at(v, HALO), at(u1, HALO)))
        for i in range(HALO, HALO + 2):
            count(4, forms(at(u1, i), at(u1, i)))
            count(6, forms(at(u1, i), at(u2, i)))
        for i in range(HALO, HALO + 3):
            count(8, forms(at(u2, i), at(u2, i)))
            count(10, forms(at(u2, i), at(u3, i)))
        for c in range(2):
            b1_ref[c, 1 if high else 0] = u1[c][HALO][:, 0:128]
            for i in range(2):
                b2_ref[c, 3 - i if high else i] = u2[c][HALO + i][:, 0:128]
        yield

    for _ in zip(end(False), end(True)):
        pass

    lane = lanes((1, 128))
    line = jnp.zeros((1, 128), jnp.float32)
    for j, part in enumerate(sums):
        line = jnp.where(lane == j, jnp.sum(part, keepdims=True), line)
    mine = shift_ref.shape[0]
    for i in range(mine):
        for c in range(2):
            for base, ref in ((SHIFT_LANE, shift_ref), (WEIGHT_LANE, weight_ref)):
                here = (lane == base + 16 * c + mine * pole + i) & (tile == 0)
                line = jnp.where(here, ref[i:i + 1, c:c + 1], line)
    line_ref[...] = jnp.broadcast_to(line, line_ref.shape)


def mul(a, b):
    return a[0] * b[0] - a[1] * b[1], a[0] * b[1] + a[1] * b[0]


def add(a, b):
    return a[0] + b[0], a[1] + b[1]


def sub(a, b):
    return a[0] - b[0], a[1] - b[1]


def over(a, b):
    norm = b[0] * b[0] + b[1] * b[1]
    factor = jnp.where(norm > 0.0, 1.0 / norm, 0.0)
    return (a[0] * b[0] + a[1] * b[1]) * factor, (a[1] * b[0] - a[0] * b[1]) * factor


def coefficients(line, poles):
    at = lanes((1, 128))

    def spot(j):
        return jnp.sum(jnp.where(at == j, line, 0.0), axis=1, keepdims=True) + jnp.zeros((1, 128), jnp.float32)

    m = [(spot(2 * j), spot(2 * j + 1)) for j in range(MOMENTS)]
    shift = tuple(pltpu.roll(line, (128 - SHIFT_LANE - 16 * c) % 128, 1) for c in range(2))
    weight = tuple(pltpu.roll(line, (128 - WEIGHT_LANE - 16 * c) % 128, 1) for c in range(2))
    scale = 1.0 / jnp.maximum(jnp.abs(m[0][0]), jnp.abs(m[0][1]))
    m = [(re * scale, im * scale) for re, im in m]
    mean = over(m[1], m[0])
    rest = list(m)
    for level in range(1, MOMENTS):
        for j in range(MOMENTS - 1, level - 1, -1):
            rest[j] = sub(rest[j], mul(mean, rest[j - 1]))
    c0, c2, c3, c4, c5 = rest[0], rest[2], rest[3], rest[4], rest[5]
    b1, e1 = over(c2, c0), over(c3, c2)
    d2 = sub(sub(c4, mul(e1, c3)), mul(b1, c2))
    b2 = over(d2, c2)
    e2 = over(sub(sub(sub(c5, mul(e1, c4)), mul(b1, c3)), mul(e1, d2)), d2)
    base = add((shift[1] / TIME_STEP + SIGMA, -shift[0] / TIME_STEP), mean)
    g2 = add(base, e2)
    g1 = sub(mul(add(base, e1), g2), b2)
    source = over((jnp.zeros_like(line), jnp.full_like(line, -1.0 / TIME_STEP)), sub(mul(base, g1), mul(b1, g2)))
    y0, y1, y2 = mul(source, g1), mul((-source[0], -source[1]), g2), source
    k1 = sub(y1, mul(e1, y2))
    k0 = sub(y0, mul(b1, y2))
    k0 = add(sub(k0, mul(mean, k1)), mul(mul(mean, mean), y2))
    twice = mul(mean, y2)
    k1 = sub(k1, (2.0 * twice[0], 2.0 * twice[1]))
    found = []
    for k in (k0, k1, y2):
        term = mul(weight, k)
        found.append(tuple(jnp.sum(jnp.where(at < poles, part, 0.0), axis=1, keepdims=True) for part in term))
    return found


def combine_kernel(poles, field_ref, u1_ref, u2_ref, b1_ref, b2_ref, sums_ref, out_ref, held, sems):
    line = jnp.sum(sums_ref[...], axis=0, keepdims=True)
    k = coefficients(line, poles)
    rows = field_ref.shape[1]
    k = [tuple(jnp.broadcast_to(part, (8, 128)) for part in pair) for pair in k]

    def source(inner, outer, reach, i):
        if i < reach:
            return outer, i
        if i >= rows - reach:
            return outer, i - rows + 2 * reach
        return inner, i

    parts = 2
    copies = []
    for i in range(rows):
        places = ((field_ref, i), source(u1_ref, b1_ref, 1, i), source(u2_ref, b2_ref, 2, i))
        for h in range(field_ref.shape[2] // 8):
            at = slice(8 * h, 8 * h + 8)
            total = None
            for pair, (ref, x) in zip(k, places):
                term = mul(pair, (ref[0, x, at, 0:128], ref[1, x, at, 0:128]))
                total = term if total is None else add(total, term)
            held[0, i, at] = total[0]
            held[1, i, at] = total[1]
        if (i + 1) % (rows // parts) == 0:
            part = pl.ds(i + 1 - rows // parts, rows // parts)
            for c in range(2):
                copy = pltpu.make_async_copy(held.at[c, part], out_ref.at[c, part], sems.at[c, len(copies) // 2])
                copy.start()
                copies.append(copy)
    for copy in copies:
        copy.wait()


def call(kernel, out_shape, specs, scratch=(), flops=0, bytes_accessed=0, aliases={}, out_spec=VMEM):
    return pl.pallas_call(
        kernel,
        out_shape=out_shape,
        in_specs=specs,
        out_specs=jax.tree.map(lambda _: out_spec, out_shape),
        scratch_shapes=list(scratch),
        input_output_aliases=aliases,
        compiler_params=pltpu.CompilerParams(vmem_limit_bytes=32 * 2**20),
        cost_estimate=pl.CostEstimate(flops=flops, bytes_accessed=bytes_accessed, transcendentals=0),
    )


def swaps(axis):
    size = lax.axis_size(axis)
    return [(i, i ^ 1) for i in range(size)], [(i, (i + 1 - 2 * (i % 2 == 0)) % size) for i in range(size)]


def on_device(psi, trap, pole_shift, pole_weight):
    tiles, poles = lax.axis_size("tile"), lax.axis_size("pole")
    rows, depth, width = trap.shape
    f32 = functools.partial(jax.ShapeDtypeStruct, dtype=jnp.float32)

    edge = f32((3 * HALO - 1, depth, width))
    s2, s1 = call(
        end_kernel, (edge, edge), [ANYWHERE] * 2,
        [pltpu.VMEM((2, 3, HALO, depth, width), jnp.float32), pltpu.SemaphoreType.DMA((2, 2))],
        flops=2_000_000_000, bytes_accessed=40_000_000,
    )(*(pltpu.with_memory_space_constraint(x, pltpu.HBM) for x in (psi, trap)))
    near, across = swaps("tile")
    pairs = []
    for pole in range(poles):
        for tile, other in across:
            pairs.append((pole * tiles + tile, (pole * tiles + other) if abs(tile - other) == 1 else ((pole ^ 1) * tiles + tile)))
    x2 = lax.ppermute(s2, ("pole", "tile"), pairs)
    x1 = lax.ppermute(s1, "tile", near)

    message = f32((3, depth, 128))
    m1, m2, field = call(
        load_kernel, (message, message, f32((3, rows, depth, width))), [VMEM] * 2,
    )(psi, trap)
    pole_near, pole_across = swaps("pole")
    y2 = lax.ppermute(m2, "pole", pole_across)
    y1 = lax.ppermute(m1, "pole", pole_near)

    wide = f32((2, rows, depth, 2 * width))
    grown, u1, sums1 = call(
        first_kernel,
        (f32((3, rows, depth, 2 * width)), wide, f32((4, 8, 128))),
        [VMEM] * 3, flops=8_000_000, bytes_accessed=3_000_000,
    )(field, y1, y2)
    x2, x1, sums1 = lax.optimization_barrier((x2, x1, sums1))
    corner = call(corner_kernel, f32((depth, 128)), [VMEM] * 2)(x2, x1)
    c2 = lax.ppermute(corner, "pole", pole_across)
    c1 = lax.ppermute(corner, "pole", pole_near)

    u2, sums2 = call(
        second_kernel, (wide, f32((8, 8, 128))), [VMEM] * 2, flops=12_000_000, bytes_accessed=5_000_000,
    )(grown, u1)

    devices = tiles * poles
    b1, b2, line = call(
        outer_kernel,
        (f32((2, 2, depth, width)), f32((2, 4, depth, width)), f32((devices, 128))),
        [VMEM] * 11,
    )(pole_shift, pole_weight, grown, u1, u2, sums1, sums2, x2, x1, c1, c2)

    lines = lax.all_to_all(line.reshape(devices, 1, 128), ("pole", "tile"), 0, 0, tiled=True)
    combine = functools.partial(combine_kernel, pole_shift.shape[0] * poles)
    return call(
        combine, f32((2, rows, depth, width)), [VMEM] * 6,
        [pltpu.VMEM((2, rows, depth, width), jnp.float32), pltpu.SemaphoreType.DMA((2, 2))], out_spec=ANYWHERE,
    )(field, u1, u2, b1, b2, lines.reshape(devices, 128))


def solution(mesh):
    placed = (
        P(None, "tile", None, "pole"),
        P("tile", None, "pole"),
        P("pole", None),
        P("pole", None),
    )
    return jax.shard_map(
        on_device,
        mesh=mesh,
        in_specs=placed,
        out_specs=P(None, "tile", None, "pole"),
        check_vma=False,
    )
```
